256 devices in a mesh: dp: 16 (over x, z_lo, core), ctx: 16 (over y, z_hi).
Axes of the slice: x: 4, y: 4, z: 8 (z_hi: 4, z_lo: 2; z = z_hi * 2 + z_lo), core: 2. Of those that a mesh axis runs over, the one named last changes fastest.
Arguments:
- queries: bfloat16 [16, 4096, 2048], P('dp', 'ctx'), may hold values from -4.5 to 4.5
- keys: bfloat16 [16, 4096, 2048], P('dp', 'ctx'), may hold values from -4.5 to 4.5
- values: bfloat16 [16, 4096, 2048], P('dp', 'ctx'), may hold values from -6 to 6
- out_grad: bfloat16 [16, 4096, 2048], P('dp', 'ctx'), may hold values from -6 to 6
- chosen: int32 [16, 16], P('dp'), may hold values from -1 to 31, as said below
- proj: bfloat16 [2048, 2048], P('ctx', 'dp'), may hold values from -0.125 to 0.125
Outputs:
- attn_out: bfloat16 [16, 4096, 2048], P('dp', 'ctx')
- q_grad: bfloat16 [16, 4096, 2048], P('dp', 'ctx')
- k_grad: bfloat16 [16, 4096, 2048], P('dp', 'ctx')
- v_grad: bfloat16 [16, 4096, 2048], P('dp', 'ctx')
- proj_grad: float32 [2048, 2048], P('ctx', 'dp')
The draws below stay inside these ranges and needn't reach their ends.
Inputs may be any that keep to these rules, and one draw needn't show every extreme that they name: chosen[d, c] is -1 or the index pos // 128 of one of the blocks that ctx index c stores (position spans c and 31 - c, of 1 block each); every sequence has one or more entries that are not -1.
All inputs are finite; a program needn't handle non-finite values.
Results may differ from the reference program's by a relative error of at most 0.023.
Values may be sent and summed in bfloat16 or wider, within the bound.
No kernel may reach another device: no remote copies, remote signals or barrier semaphores. Data moves between devices by JAX's collectives and lax.ppermute only.
A program may use at most 192 MiB of HBM per device.

```python
import math
import jax
import jax.numpy as jnp
from jax import lax

DH = 128
DOUT = 2048
BLOCK = 128
SPAN_BLOCKS = 1
HEADS = 16
HD = 2048
TOK_DEV = 256
SEQ = 4096
SLOTS = 2048
N_DP = 16
N_CTX = 16


def base_field(key, salt):
    inner = jax.random.fold_in(key, salt)
    field = jnp.clip(jax.random.normal(inner, (N_DP, SEQ, HD)), -4.5, 4.5)
    return field


def draw_queries(key, part):
    field = base_field(key, 1)
    return field.astype(jnp.bfloat16)


def draw_keys(key, part):
    field = base_field(key, 2)
    return field.astype(jnp.bfloat16)


def draw_chosen(key, part):
    ctx_ids = jnp.arange(N_CTX, dtype=jnp.int32)[None, :]
    pick = jax.random.randint(jax.random.fold_in(key, 11), (N_DP, N_CTX), 0, 2 * SPAN_BLOCKS)
    span_id = jnp.where(pick < SPAN_BLOCKS, ctx_ids, 2 * N_CTX - 1 - ctx_ids)
    block_id = span_id * SPAN_BLOCKS + pick % SPAN_BLOCKS
    active = jax.random.randint(jax.random.fold_in(key, 12), (N_DP, N_CTX), 0, 5) < 3
    forced = jax.random.randint(jax.random.fold_in(key, 13), (N_DP, 1), 0, N_CTX)
    active = active | (ctx_ids == forced)
    return jnp.where(active, block_id, -1).astype(jnp.int32)


def with_spikes(drawn, stream_key, source, target, blocks, factor):
    def block_of(position):
        return (jnp.arange(drawn.shape[position]) // (drawn.shape[position] // blocks)).reshape((-1,) + (1,) * (drawn.ndim - 1 - position))

    first = jax.random.permutation(stream_key, blocks)[block_of(target)]
    second = (block_of(target) + blocks // 2) % blocks
    return jnp.where((block_of(source) == first) | (block_of(source) == second), factor * drawn, drawn)


def shard_levels(own_key, extent, pieces, low, top_value):
    loudness, own = 1.0, jax.random.fold_in(own_key, 6)
    for axis_at, parts in pieces:
        draws = jnp.exp(jax.random.uniform(jax.random.fold_in(own, axis_at), (parts,), jnp.float32, low / len(pieces), top_value / len(pieces)))
        loudness = loudness * jnp.repeat(draws, extent[axis_at] // parts).reshape([-1 if axis == axis_at else 1 for axis in range(len(extent))])
    return loudness


def noise(own_key, dims, spread, reach, shards=(), held_as=jnp.bfloat16):
    loudness = shard_levels(own_key, dims, shards, -0.22, 0.18) if shards else 1.0
    drawn = jax.random.normal(own_key, dims, jnp.float32) * spread * loudness
    return jnp.minimum(jnp.maximum(drawn, -reach), reach).astype(held_as)


def heavy_noise(own_key, dims, width, limit, cuts, heavy, kind=jnp.bfloat16):
    drawn = width * jax.random.normal(own_key, dims, jnp.float32)
    if cuts:
        drawn = drawn * shard_levels(own_key, dims, cuts, -0.22, 0.18)
    return jnp.clip(with_spikes(drawn, jax.random.fold_in(own_key, 3), *heavy), -limit, limit).astype(kind)


def setup_inputs(seed: int = 0) -> dict:
    key_of = jax.random.split(jax.random.key(seed), 7)
    queries = draw_queries(jax.random.fold_in(key_of[6], 71), 0)
    keys = draw_keys(jax.random.fold_in(key_of[6], 71), 0)
    values = noise(key_of[2], (N_DP, SEQ, HD), 1.0, 6.0, ((0, 16), (1, 16)))
    out_grad = heavy_noise(key_of[3], (N_DP, SEQ, DOUT), 1.0, 6.0, ((0, 16), (1, 16)), (0, 2, 16, 2.0))
    chosen = draw_chosen(jax.random.fold_in(key_of[6], 71), 0)
    proj = noise(key_of[5], (HD, DOUT), HD ** -0.5, 0.125, ((0, 16), (1, 16)))
    return dict(queries=queries, keys=keys, values=values, out_grad=out_grad, chosen=chosen, proj=proj)


def slot_rows(picked):
    half_rows = TOK_DEV // 2
    ctx_ids = jnp.arange(N_CTX, dtype=jnp.int32)
    live_pick = picked >= 0
    safe_pick = jnp.where(live_pick, picked, 0).astype(jnp.int32)
    first_pos = safe_pick * BLOCK
    span_id = first_pos // half_rows
    local_row = jnp.where(span_id == ctx_ids, first_pos % half_rows, half_rows + first_pos % half_rows)
    local_row = jnp.where(live_pick, local_row, 0).astype(jnp.int32)
    offsets = jnp.arange(BLOCK, dtype=jnp.int32)
    src_rows = (ctx_ids[:, None] * TOK_DEV + local_row[:, None] + offsets[None, :]).reshape(SLOTS).astype(jnp.int32)
    slot_pos = (safe_pick[:, None] * BLOCK + offsets[None, :]).reshape(SLOTS).astype(jnp.int32)
    slot_live = jnp.repeat(live_pick, BLOCK)
    return (src_rows, slot_pos, slot_live)

def head_probs(head_q, head_k, allowed):
    scores = jnp.dot(head_q, head_k.T, preferred_element_type=jnp.float32) * (1.0 / math.sqrt(DH))
    masked = jnp.where(allowed, scores, -1e+30)
    row_max = lax.optimization_barrier(jnp.max(masked, axis=1, keepdims=True))
    exp_terms = jnp.where(allowed, jnp.exp(masked - row_max), 0.0)
    return exp_terms / lax.optimization_barrier(jnp.sum(exp_terms, axis=1, keepdims=True))

def head_forward(head_q, head_k, head_v, allowed):
    attn_prob = head_probs(head_q, head_k, allowed)
    return jnp.dot(attn_prob.astype(jnp.bfloat16), head_v, preferred_element_type=jnp.float32).astype(jnp.bfloat16)

def head_backward(head_q, head_k, head_v, head_a, head_g, allowed):
    attn_prob = head_probs(head_q, head_k, allowed)
    prob_b = attn_prob.astype(jnp.bfloat16)
    row_delta = lax.optimization_barrier(jnp.sum(head_g.astype(jnp.float32) * head_a.astype(jnp.float32), axis=1, keepdims=True))
    prob_grad = jnp.dot(head_g, head_v.T, preferred_element_type=jnp.float32)
    score_grad = (attn_prob * (prob_grad - row_delta)).astype(jnp.bfloat16)
    score_scale = 1.0 / math.sqrt(DH)
    grad_q = (jnp.dot(score_grad, head_k, preferred_element_type=jnp.float32) * score_scale).astype(jnp.bfloat16)
    grad_k = (jnp.dot(score_grad.T, head_q, preferred_element_type=jnp.float32) * score_scale).astype(jnp.bfloat16)
    grad_v = jnp.dot(prob_b.T, head_g, preferred_element_type=jnp.float32).astype(jnp.bfloat16)
    return (grad_q, grad_k, grad_v)

def split_heads(block_rows):
    return block_rows.reshape(SLOTS, HEADS, DH).transpose(1, 0, 2)

def join_heads(block_rows):
    return block_rows.transpose(1, 0, 2).reshape(SLOTS, HD)

def one_sequence(seq_query, seq_key, seq_value, seq_grad, picked, proj):
    src_rows, slot_pos, slot_live = slot_rows(picked)
    live_col = slot_live[:, None]
    zero_bf = jnp.zeros((), jnp.bfloat16)
    query_slots = jnp.where(live_col, seq_query[src_rows], zero_bf)
    key_slots = jnp.where(live_col, seq_key[src_rows], zero_bf)
    value_slots = jnp.where(live_col, seq_value[src_rows], zero_bf)
    grad_slots = jnp.where(live_col, seq_grad[src_rows], zero_bf)
    slot_ids = jnp.arange(SLOTS, dtype=jnp.int32)
    allowed = live_col & slot_live[None, :] & (slot_pos[None, :] <= slot_pos[:, None]) | (slot_ids[:, None] == slot_ids[None, :])
    heads_q = split_heads(query_slots)
    heads_k = split_heads(key_slots)
    heads_v = split_heads(value_slots)

    def forward_one(triple):
        return head_forward(triple[0], triple[1], triple[2], allowed)
    attn_heads = lax.map(forward_one, (heads_q, heads_k, heads_v))
    attn = join_heads(attn_heads)
    mixed = jnp.dot(attn, proj, preferred_element_type=jnp.float32).astype(jnp.bfloat16)
    attn_grad = jnp.dot(grad_slots, proj.T, preferred_element_type=jnp.float32).astype(jnp.bfloat16)
    weight_term = jnp.dot(attn.T, grad_slots, preferred_element_type=jnp.float32)

    def backward_one(group):
        return head_backward(group[0], group[1], group[2], group[3], group[4], allowed)
    grad_q, grad_k, grad_v = lax.map(backward_one, (heads_q, heads_k, heads_v, attn_heads, split_heads(attn_grad)))
    out_rows = jnp.zeros((SEQ, DOUT), jnp.bfloat16).at[src_rows].set(mixed)
    blank = jnp.zeros((SEQ, HD), jnp.bfloat16)
    q_rows = blank.at[src_rows].set(join_heads(grad_q))
    k_rows = blank.at[src_rows].set(join_heads(grad_k))
    v_rows = blank.at[src_rows].set(join_heads(grad_v))
    return ((out_rows, q_rows, k_rows, v_rows), weight_term)

def reference(queries, keys, values, out_grad, chosen, proj):

    def scan_step(total, inputs):
        results, weight_term = one_sequence(inputs[0], inputs[1], inputs[2], inputs[3], inputs[4], proj)
        return (total + weight_term, results)
    total, stacked = lax.scan(scan_step, jnp.zeros((HD, DOUT), jnp.float32), (queries, keys, values, out_grad, chosen))
    return (stacked[0], stacked[1], stacked[2], stacked[3], total)
```

```python
import math

import jax
import jax.numpy as jnp
from jax import lax
from jax.experimental import pallas as pl
from jax.experimental.pallas import tpu as pltpu
from jax.sharding import PartitionSpec as P

BLK = 128
Y = 4
Z = 4
NC = Y * Z
Y_GROUPS = [[y * Z + z for y in range(Y)] for z in range(Z)]
Z_GROUPS = [[y * Z + z for z in range(Z)] for y in range(Y)]
PAIR = 2 * BLK
NEG = -1e30
VMEM_BYTES = 48 * 1024 * 1024
F32 = jnp.float32
BF16 = jnp.bfloat16


def dot_nt(a, b):
    return lax.dot_general(a, b, (((1,), (1,)), ((), ())), preferred_element_type=F32)


def dot_nn(a, b):
    return lax.dot_general(a, b, (((1,), (0,)), ((), ())), preferred_element_type=F32)


def params():
    return pltpu.CompilerParams(vmem_limit_bytes=VMEM_BYTES)


def cost(flops, nbytes, trans=0):
    return pl.CostEstimate(flops=flops, bytes_accessed=nbytes, transcendentals=trans)


def take_body(where_ref, q_ref, k_ref, v_ref, g_ref, qkv_ref, gs_ref):
    live = where_ref[1] > 0
    zero = jnp.zeros((), BF16)
    heads = qkv_ref.shape[0]
    for h in range(heads):
        cols = slice(h * BLK, (h + 1) * BLK)
        for part, src in enumerate((q_ref, k_ref, v_ref)):
            qkv_ref[h, part * BLK : (part + 1) * BLK, :] = jnp.where(live, src[0, :, cols], zero)
    gs_ref[...] = jnp.where(live, g_ref[0], zero)


def take_rows(where, queries, keys, values, out_grad):
    feats = queries.shape[2]
    steps = 4
    width = feats // steps
    src = pl.BlockSpec((1, BLK, width), lambda i, w: (0, w[0], i))
    return pl.pallas_call(
        take_body,
        grid_spec=pltpu.PrefetchScalarGridSpec(
            num_scalar_prefetch=1,
            grid=(steps,),
            in_specs=[src] * 4,
            out_specs=[
                pl.BlockSpec((NC // steps, 3 * BLK, BLK), lambda i, w: (i, 0, 0)),
                pl.BlockSpec((BLK, width), lambda i, w: (0, i)),
            ],
        ),
        out_shape=[
            jax.ShapeDtypeStruct((NC, 3 * BLK, BLK), BF16),
            jax.ShapeDtypeStruct((BLK, feats), BF16),
        ],
        compiler_params=params(),
        cost_estimate=cost(0, 8 * BLK * feats * 2),
        name="take_rows",
    )(where, queries, keys, values, out_grad)


def attn_grad_body(g_ref, w_ref, out_ref, wide_ref):
    nd = w_ref.shape[0]
    for d in range(nd):
        for b in range(Z):
            wide_ref[b * BLK : (b + 1) * BLK, d * BLK : (d + 1) * BLK] = w_ref[d, b]
    for b in range(Z):
        for a in range(Y):
            out_ref[b, a] = dot_nt(g_ref[a], wide_ref[b * BLK : (b + 1) * BLK, :]).astype(BF16)


def attn_grad_product(gs_y, proj_rows):
    cols = gs_y.shape[2]
    return pl.pallas_call(
        attn_grad_body,
        out_shape=[
            jax.ShapeDtypeStruct((Z, Y, BLK, BLK), BF16),
            jax.ShapeDtypeStruct((Z * BLK, cols), BF16),
        ],
        compiler_params=params(),
        cost_estimate=cost(2 * 512 * 512 * cols, 3 * 512 * cols * 2),
        name="attn_grad_product",
    )(gs_y, proj_rows)


def sort_blocks(chosen_ref, order_ref):
    count = jnp.int32(0)
    for pos in range(2 * NC):
        c = pos if pos < NC else 2 * NC - 1 - pos
        hit = chosen_ref[c] == pos

        @pl.when(hit)
        def _():
            order_ref[count] = c

        count = count + hit.astype(jnp.int32)
    live = count
    for c in range(NC):
        hit = chosen_ref[c] < 0

        @pl.when(hit)
        def _():
            order_ref[count] = c

        count = count + hit.astype(jnp.int32)
    return live


def causal(s):
    key = lax.broadcasted_iota(jnp.int32, s.shape, 0)
    query = lax.broadcasted_iota(jnp.int32, s.shape, 1)
    return jnp.where(key <= query, s, NEG)


def forward_body(chosen_ref, qkv_ref, attn_ref, lse_ref, q_s, k_s, vt_s, order_ref):
    live = sort_blocks(chosen_ref, order_ref)
    scale2 = math.log2(math.e) / math.sqrt(BLK)
    for r in range(NC):
        c = order_ref[r]
        rows = slice(r * BLK, (r + 1) * BLK)

        @pl.when(r // 2 * 2 < live)
        def _():
            q_s[rows, :] = qkv_ref[c, 0:BLK, :]
            k_s[rows, :] = qkv_ref[c, BLK : 2 * BLK, :]
            vt_s[:, rows] = qkv_ref[c, 2 * BLK : 3 * BLK, :].T

        @pl.when(r >= live)
        def _():
            attn_ref[c % Z, c // Z] = jnp.zeros((BLK, BLK), BF16)

    for p in range(NC // 2):

        @pl.when(2 * p < live)
        def _():
            low = p * PAIR
            q2 = q_s[low : low + PAIR, :]
            diag = causal(dot_nt(k_s[low : low + PAIR, :], q2))
            parts = [(low, diag)]
            top = jnp.max(diag, axis=0, keepdims=True)
            for j in range(p):
                s = dot_nt(k_s[j * PAIR : (j + 1) * PAIR, :], q2)
                top = jnp.maximum(top, jnp.max(s, axis=0, keepdims=True))
                parts.append((j * PAIR, s))
            total = jnp.zeros((1, PAIR), F32)
            out_t = jnp.zeros((BLK, PAIR), F32)
            shift = top * scale2
            for start, s in parts:
                e = jnp.exp2(s * scale2 - shift)
                total = total + jnp.sum(e, axis=0, keepdims=True)
                out_t = out_t + dot_nn(vt_s[:, start : start + PAIR], e.astype(BF16))
            lse_ref[p : p + 1, :] = shift + jnp.log2(total)
            out = (out_t * (1.0 / total)).T.astype(BF16)
            for t in range(2):
                c = order_ref[2 * p + t]

                @pl.when(2 * p + t < live)
                def _():
                    attn_ref[c % Z, c // Z] = out[t * BLK : (t + 1) * BLK, :]


def attn_forward(chosen, qkv):
    slots = NC * BLK
    return pl.pallas_call(
        forward_body,
        in_specs=[
            pl.BlockSpec(memory_space=pltpu.SMEM),
            pl.BlockSpec(memory_space=pltpu.VMEM),
        ],
        out_shape=[
            jax.ShapeDtypeStruct((Z, Y, BLK, BLK), BF16),
            jax.ShapeDtypeStruct((NC // 2, PAIR), F32),
        ],
        scratch_shapes=[
            pltpu.VMEM((slots, BLK), BF16),
            pltpu.VMEM((slots, BLK), BF16),
            pltpu.VMEM((BLK, slots), BF16),
            pltpu.SMEM((NC,), jnp.int32),
        ],
        compiler_params=params(),
        cost_estimate=cost(2 * 2 * slots * slots * BLK, 4 * slots * BLK * 2, slots * slots),
        name="attn_forward",
    )(chosen, qkv)


def backward_body(
    chosen_ref,
    qkv_ref,
    grad_ref,
    attn_ref,
    lse_ref,
    out_ref,
    q_s,
    k_s,
    v_s,
    g_s,
    kt_s,
    dk_s,
    dv_s,
    order_ref,
):
    live = sort_blocks(chosen_ref, order_ref)
    scale = 1.0 / math.sqrt(BLK)
    scale2 = math.log2(math.e) * scale
    for r in range(NC):
        c = order_ref[r]
        rows = slice(r * BLK, (r + 1) * BLK)

        @pl.when(r // 2 * 2 < live)
        def _():
            k_blk = qkv_ref[c, BLK : 2 * BLK, :]
            q_s[rows, :] = qkv_ref[c, 0:BLK, :]
            k_s[rows, :] = k_blk
            kt_s[:, rows] = k_blk.T
            v_s[rows, :] = qkv_ref[c, 2 * BLK : 3 * BLK, :]
            g_s[rows, :] = grad_ref[c % Z, c // Z]

        @pl.when(r >= live)
        def _():
            out_ref[c] = jnp.zeros((3 * BLK, BLK), BF16)

    for p in range(NC // 2):

        @pl.when(2 * p < live)
        def _():
            low = p * PAIR
            q2 = q_s[low : low + PAIR, :]
            g2 = g_s[low : low + PAIR, :]
            deltas = []
            for t in range(2):
                c = order_ref[2 * p + t]
                prod = g2[t * BLK : (t + 1) * BLK, :].astype(F32) * attn_ref[c % Z, c // Z].astype(F32)
                deltas.append(jnp.sum(prod.T, axis=0, keepdims=True))
            delta = jnp.concatenate(deltas, axis=1)
            lse = lse_ref[p : p + 1, :]
            dq_t = jnp.zeros((BLK, PAIR), F32)
            for j in range(p + 1):
                keys = slice(j * PAIR, (j + 1) * PAIR)
                s = dot_nt(k_s[keys, :], q2)
                if j == p:
                    s = causal(s)
                prob = jnp.exp2(s * scale2 - lse)
                dprob = dot_nt(v_s[keys, :], g2)
                ds = (prob * (dprob - delta)).astype(BF16)
                dv = dot_nn(prob.astype(BF16), g2)
                dk = dot_nn(ds, q2)
                if j == p:
                    dv_s[keys, :] = dv
                    dk_s[keys, :] = dk
                else:
                    dv_s[keys, :] += dv
                    dk_s[keys, :] += dk
                dq_t = dq_t + dot_nn(kt_s[:, keys], ds)
            dq = (dq_t * scale).T.astype(BF16)
            for t in range(2):
                c = order_ref[2 * p + t]

                @pl.when(2 * p + t < live)
                def _():
                    out_ref[c, 0:BLK, :] = dq[t * BLK : (t + 1) * BLK, :]

    for r in range(NC):
        c = order_ref[r]
        rows = slice(r * BLK, (r + 1) * BLK)

        @pl.when(r < live)
        def _():
            out_ref[c, BLK : 2 * BLK, :] = (dk_s[rows, :] * scale).astype(BF16)
            out_ref[c, 2 * BLK : 3 * BLK, :] = dv_s[rows, :].astype(BF16)


def attn_backward(chosen, qkv, grad, attn, lse):
    slots = NC * BLK
    return pl.pallas_call(
        backward_body,
        in_specs=[pl.BlockSpec(memory_space=pltpu.SMEM)] + [pl.BlockSpec(memory_space=pltpu.VMEM)] * 4,
        out_shape=jax.ShapeDtypeStruct((NC, 3 * BLK, BLK), BF16),
        scratch_shapes=[
            pltpu.VMEM((slots, BLK), BF16),
            pltpu.VMEM((slots, BLK), BF16),
            pltpu.VMEM((slots, BLK), BF16),
            pltpu.VMEM((slots, BLK), BF16),
            pltpu.VMEM((BLK, slots), BF16),
            pltpu.VMEM((slots, BLK), F32),
            pltpu.VMEM((slots, BLK), F32),
            pltpu.SMEM((NC,), jnp.int32),
        ],
        compiler_params=params(),
        cost_estimate=cost(5 * 2 * slots * slots * BLK, 8 * slots * BLK * 2, slots * slots),
        name="attn_backward",
    )(chosen, qkv, grad, attn, lse)


def proj_body(attn_ref, wide_ref, g_ref, mix_ref, dw_ref, a_s, at_s):
    @pl.when(pl.program_id(0) == 0)
    def _():
        for b in range(Z):
            for a in range(Y):
                blk = attn_ref[b, a]
                a_s[a * BLK : (a + 1) * BLK, b * BLK : (b + 1) * BLK] = blk
                at_s[b * BLK : (b + 1) * BLK, a * BLK : (a + 1) * BLK] = blk.T

    width = wide_ref.shape[1]
    for a in range(Y):
        mix_ref[a] = dot_nn(a_s[a * BLK : (a + 1) * BLK, :], wide_ref[...]).astype(BF16)
    grads = g_ref[...].reshape(Y * BLK, width)
    for b in range(Z):
        part = dot_nn(at_s[b * BLK : (b + 1) * BLK, :], grads).astype(BF16)
        for d in range(width // BLK):
            dw_ref[d, b] = part[:, d * BLK : (d + 1) * BLK]


def proj_products(attn_p, wide, gs_y):
    cols = wide.shape[1]
    steps = 4
    width = cols // steps
    return pl.pallas_call(
        proj_body,
        grid=(steps,),
        in_specs=[
            pl.BlockSpec((Z, Y, BLK, BLK), lambda i: (0, 0, 0, 0)),
            pl.BlockSpec((Z * BLK, width), lambda i: (0, i)),
            pl.BlockSpec((Y, BLK, width), lambda i: (0, 0, i)),
        ],
        out_specs=[
            pl.BlockSpec((Y, BLK, width), lambda i: (0, 0, i)),
            pl.BlockSpec((width // BLK, Z, BLK, BLK), lambda i: (i, 0, 0, 0)),
        ],
        out_shape=[
            jax.ShapeDtypeStruct((Y, BLK, cols), BF16),
            jax.ShapeDtypeStruct((cols // BLK, Z, BLK, BLK), BF16),
        ],
        scratch_shapes=[
            pltpu.VMEM((Y * BLK, Z * BLK), BF16),
            pltpu.VMEM((Z * BLK, Y * BLK), BF16),
        ],
        compiler_params=params(),
        cost_estimate=cost(2 * 2 * 512 * 512 * cols, 4 * 512 * cols * 2),
        name="proj_products",
    )(attn_p, wide, gs_y)


def place_mixed_body(where_ref, part_ref, out_ref):
    mine = pl.program_id(0) == where_ref[0]

    @pl.when(mine)
    def _():
        total = part_ref[0].astype(F32)
        for a in range(1, Y):
            total = total + part_ref[a].astype(F32)
        out_ref[0] = total.astype(BF16)

    @pl.when(jnp.logical_not(mine))
    def _():
        out_ref[...] = jnp.zeros(out_ref.shape, BF16)


def place_mixed(where, parts):
    cols = parts.shape[2]
    steps = 2
    width = cols // steps
    return pl.pallas_call(
        place_mixed_body,
        grid_spec=pltpu.PrefetchScalarGridSpec(
            num_scalar_prefetch=1,
            grid=(2, steps),
            in_specs=[pl.BlockSpec((Y, BLK, width), lambda i, j, w: (0, 0, j))],
            out_specs=pl.BlockSpec((1, BLK, width), lambda i, j, w: (0, i, j)),
        ),
        out_shape=jax.ShapeDtypeStruct((1, 2 * BLK, cols), BF16),
        compiler_params=params(),
        cost_estimate=cost(0, 6 * BLK * cols * 2),
        name="place_mixed",
    )(where, parts)


def place_grads_body(where_ref, back_ref, q_ref, k_ref, v_ref):
    mine = pl.program_id(0) == where_ref[0]
    heads = back_ref.shape[0]

    @pl.when(mine)
    def _():
        for h in range(heads):
            cols = slice(h * BLK, (h + 1) * BLK)
            for part, out in enumerate((q_ref, k_ref, v_ref)):
                out[0, :, cols] = back_ref[h, part * BLK : (part + 1) * BLK, :]

    @pl.when(jnp.logical_not(mine))
    def _():
        for out in (q_ref, k_ref, v_ref):
            out[...] = jnp.zeros(out.shape, BF16)


def place_grads(where, back):
    feats = NC * BLK
    steps = 2
    width = feats // steps
    out = pl.BlockSpec((1, BLK, width), lambda i, j, w: (0, i, j))
    shape = jax.ShapeDtypeStruct((1, 2 * BLK, feats), BF16)
    return pl.pallas_call(
        place_grads_body,
        grid_spec=pltpu.PrefetchScalarGridSpec(
            num_scalar_prefetch=1,
            grid=(2, steps),
            in_specs=[pl.BlockSpec((NC // steps, 3 * BLK, BLK), lambda i, j, w: (j, 0, 0))],
            out_specs=[out] * 3,
        ),
        out_shape=[shape] * 3,
        compiler_params=params(),
        cost_estimate=cost(0, 9 * BLK * feats * 2),
        name="place_grads",
    )(where, back)


def shards(queries, keys, values, out_grad, chosen, proj):
    picked = chosen[0]
    ctx_index = lax.axis_index("ctx")
    own_pick = lax.dynamic_index_in_dim(picked, ctx_index, 0, keepdims=False)
    own_live = own_pick >= 0
    second = own_live & (own_pick != ctx_index)
    where = jnp.stack([second, own_live]).astype(jnp.int32)

    rows_z = lax.all_gather(proj, "ctx", axis=0, axis_index_groups=Z_GROUPS)
    proj_rows = lax.all_gather(rows_z, "dp", axis=0)

    qkv_own, gs = take_rows(where, queries, keys, values, out_grad)
    gs_y = lax.all_gather(gs, "ctx", axis=0, axis_index_groups=Y_GROUPS)
    qkv = lax.all_to_all(qkv_own, "ctx", 0, 0, tiled=True)

    grad_p, wide = attn_grad_product(gs_y, proj_rows)
    grad = lax.all_to_all(grad_p, "ctx", 0, 0, tiled=True, axis_index_groups=Z_GROUPS)

    attn, lse = attn_forward(picked, qkv)
    attn_p = lax.all_to_all(attn, "ctx", 0, 0, tiled=True, axis_index_groups=Z_GROUPS)

    back = attn_backward(picked, qkv, grad, attn, lse)
    back = lax.all_to_all(back, "ctx", 0, 0, tiled=True)

    mix_p, dw_p = proj_products(attn_p, wide, gs_y)
    mix_p = lax.all_to_all(mix_p, "ctx", 0, 0, tiled=True, axis_index_groups=Y_GROUPS)
    dw_p = lax.all_to_all(dw_p, "dp", 0, 0, tiled=True)
    dw = jnp.sum(dw_p.astype(F32), axis=0)
    dw = lax.all_to_all(dw, "ctx", 0, 0, tiled=True, axis_index_groups=Z_GROUPS)
    proj_grad = jnp.sum(dw, axis=0)

    attn_out = place_mixed(where, mix_p)
    q_grad, k_grad, v_grad = place_grads(where, back)
    return attn_out, q_grad, k_grad, v_grad, proj_grad


def solution(mesh):
    rows = P("dp", "ctx", None)
    return jax.shard_map(
        shards,
        mesh=mesh,
        in_specs=(rows, rows, rows, rows, P("dp", None), P("ctx", "dp")),
        out_specs=(rows, rows, rows, rows, P("ctx", "dp")),
        check_vma=False,
    )
```

```python
import functools
import math

import jax
import jax.numpy as jnp
from jax import lax
from jax.experimental import pallas as pl
from jax.experimental.pallas import tpu as pltpu
from jax.sharding import PartitionSpec as P

BLK = 128
Y = 4
Z = 4
NC = Y * Z
PAIR = 2 * BLK
NEG = -1e30
VMEM_BYTES = 48 * 1024 * 1024
F32 = jnp.float32
BF16 = jnp.bfloat16


def dot_nt(a, b):
    return lax.dot_general(a, b, (((1,), (1,)), ((), ())), preferred_element_type=F32)


def dot_nn(a, b):
    return lax.dot_general(a, b, (((1,), (0,)), ((), ())), preferred_element_type=F32)


def params():
    return pltpu.CompilerParams(vmem_limit_bytes=VMEM_BYTES)


def cost(flops, nbytes, trans=0):
    return pl.CostEstimate(flops=flops, bytes_accessed=nbytes, transcendentals=trans)


def half_of(here_ref, chosen_ref):
    pick = chosen_ref[here_ref[0]]
    return ((pick >= 0) & (pick != here_ref[0])).astype(jnp.int32)


def take_body(here_ref, chosen_ref, q_ref, k_ref, v_ref, g_ref, qkv_ref, gs_ref):
    live = chosen_ref[here_ref[0]] >= 0
    zero = jnp.zeros((), BF16)
    heads = qkv_ref.shape[0]
    for h in range(heads):
        cols = slice(h * BLK, (h + 1) * BLK)
        for part, src in enumerate((q_ref, k_ref, v_ref)):
            qkv_ref[h, part * BLK : (part + 1) * BLK, :] = jnp.where(live, src[0, :, cols], zero)
    gs_ref[...] = jnp.where(live, g_ref[0], zero)


def take_rows(here, chosen, queries, keys, values, out_grad):
    feats = queries.shape[2]
    steps = 4
    width = feats // steps
    src = pl.BlockSpec((1, BLK, width), lambda i, h, c: (0, half_of(h, c), i))
    return pl.pallas_call(
        take_body,
        grid_spec=pltpu.PrefetchScalarGridSpec(
            num_scalar_prefetch=2,
            grid=(steps,),
            in_specs=[src] * 4,
            out_specs=[
                pl.BlockSpec((NC // steps, 3 * BLK, BLK), lambda i, h, c: (i, 0, 0)),
                pl.BlockSpec((BLK, width), lambda i, h, c: (0, i)),
            ],
        ),
        out_shape=[
            jax.ShapeDtypeStruct((NC, 3 * BLK, BLK), BF16),
            jax.ShapeDtypeStruct((BLK, feats), BF16),
        ],
        compiler_params=pltpu.CompilerParams(vmem_limit_bytes=62 * 1024 * 1024),
        cost_estimate=cost(0, 8 * BLK * feats * 2),
        name="take_rows",
    )(here, chosen, queries, keys, values, out_grad)


def join_body(*refs):
    parts, out_ref = refs[:8], refs[9]
    for i, part in enumerate(parts):
        out_ref[i] = part[...]


def join_rows(parts, passed):
    vmem = pl.BlockSpec(memory_space=pltpu.VMEM)
    anywhere = pl.BlockSpec(memory_space=pl.ANY)
    return pl.pallas_call(
        join_body,
        in_specs=[vmem] * 8 + [anywhere],
        out_specs=[vmem, anywhere],
        out_shape=[
            jax.ShapeDtypeStruct((8, BLK, BLK), BF16),
            jax.ShapeDtypeStruct(passed.shape, passed.dtype),
        ],
        input_output_aliases={8: 1},
        compiler_params=params(),
        cost_estimate=cost(0, 16 * BLK * BLK * 2),
        name="join_rows",
    )(*parts, passed)


def attn_grad_body(here_ref, *refs):
    g_refs, w_refs, outs, wide_ref = refs[:Y], refs[Y : 2 * Y], refs[2 * Y : 2 * Y + Z], refs[-1]
    x, k = here_ref[4], here_ref[5]
    for u in range(4):
        for v in range(4):
            d = (x ^ u) * 4 + (k ^ v)
            cols = pl.ds(pl.multiple_of(d * BLK, BLK), BLK)
            for t in range(Z):
                wide_ref[t * BLK : (t + 1) * BLK, cols] = w_refs[u][(v % 2) * 8 + t * 2 + v // 2]
    for t in range(Z):
        for s in range(Y):
            outs[t][s] = dot_nt(g_refs[s][...], wide_ref[t * BLK : (t + 1) * BLK, :]).astype(BF16)


def attn_grad_product(here, grads, proj_rows):
    cols = grads[0].shape[1]
    vmem = pl.BlockSpec(memory_space=pltpu.VMEM)
    return pl.pallas_call(
        attn_grad_body,
        in_specs=[pl.BlockSpec(memory_space=pltpu.SMEM)] + [vmem] * 8,
        out_shape=[jax.ShapeDtypeStruct((Y, BLK, BLK), BF16)] * Z
        + [jax.ShapeDtypeStruct((Z * BLK, cols), BF16)],
        compiler_params=params(),
        cost_estimate=cost(2 * 512 * 512 * cols, 3 * 512 * cols * 2),
        name="attn_grad_product",
    )(here, *grads, *proj_rows)


def sort_blocks(chosen_ref, order_ref):
    count = jnp.int32(0)
    for pos in range(2 * NC):
        c = pos if pos < NC else 2 * NC - 1 - pos
        hit = chosen_ref[c] == pos

        @pl.when(hit)
        def _():
            order_ref[count] = c

        count = count + hit.astype(jnp.int32)
    live = count
    for c in range(NC):
        hit = chosen_ref[c] < 0

        @pl.when(hit)
        def _():
            order_ref[count] = c

        count = count + hit.astype(jnp.int32)
    return live


def causal(s):
    key = lax.broadcasted_iota(jnp.int32, s.shape, 0)
    query = lax.broadcasted_iota(jnp.int32, s.shape, 1)
    return jnp.where(key <= query, s, NEG)


def forward_body(
    here_ref, chosen_ref, qkv_ref, attn_ref, out0, out1, out2, out3, lse_ref, q_s, k_s, vt_s, order_ref
):
    a, b = here_ref[2], here_ref[3]
    live = sort_blocks(chosen_ref, order_ref)
    scale2 = math.log2(math.e) / math.sqrt(BLK)
    for r in range(NC):
        c = order_ref[r]
        rows = slice(r * BLK, (r + 1) * BLK)

        @pl.when(r // 2 * 2 < live)
        def _():
            q_s[rows, :] = qkv_ref[c, 0:BLK, :]
            k_s[rows, :] = qkv_ref[c, BLK : 2 * BLK, :]
            vt_s[:, rows] = qkv_ref[c, 2 * BLK : 3 * BLK, :].T

        @pl.when(r >= live)
        def _():
            attn_ref[b ^ (c % Z), a ^ (c // Z)] = jnp.zeros((BLK, BLK), BF16)

    for p in range(NC // 2):

        @pl.when(2 * p < live)
        def _():
            low = p * PAIR
            q2 = q_s[low : low + PAIR, :]
            diag = causal(dot_nt(k_s[low : low + PAIR, :], q2))
            parts = [(low, diag)]
            top = jnp.max(diag, axis=0, keepdims=True)
            for j in range(p):
                s = dot_nt(k_s[j * PAIR : (j + 1) * PAIR, :], q2)
                top = jnp.maximum(top, jnp.max(s, axis=0, keepdims=True))
                parts.append((j * PAIR, s))
            total = jnp.zeros((1, PAIR), F32)
            out_t = jnp.zeros((BLK, PAIR), F32)
            shift = top * scale2
            for start, s in parts:
                e = jnp.exp2(s * scale2 - shift)
                total = total + jnp.sum(e, axis=0, keepdims=True)
                out_t = out_t + dot_nn(vt_s[:, start : start + PAIR], e.astype(BF16))
            lse_ref[p : p + 1, :] = shift + jnp.log2(total)
            out = (out_t * (1.0 / total)).T.astype(BF16)
            for t in range(2):
                c = order_ref[2 * p + t]

                @pl.when(2 * p + t < live)
                def _():
                    attn_ref[b ^ (c % Z), a ^ (c // Z)] = out[t * BLK : (t + 1) * BLK, :]

    for t, out_ref in enumerate((out0, out1, out2, out3)):
        out_ref[...] = attn_ref[t]


def attn_forward(here, chosen, qkv):
    slots = NC * BLK
    return pl.pallas_call(
        forward_body,
        in_specs=[
            pl.BlockSpec(memory_space=pltpu.SMEM),
            pl.BlockSpec(memory_space=pltpu.SMEM),
            pl.BlockSpec(memory_space=pltpu.VMEM),
        ],
        out_shape=[jax.ShapeDtypeStruct((Z, Y, BLK, BLK), BF16)]
        + [jax.ShapeDtypeStruct((Y, BLK, BLK), BF16)] * Z
        + [
            jax.ShapeDtypeStruct((NC // 2, PAIR), F32),
        ],
        scratch_shapes=[
            pltpu.VMEM((slots, BLK), BF16),
            pltpu.VMEM((slots, BLK), BF16),
            pltpu.VMEM((BLK, slots), BF16),
            pltpu.SMEM((NC,), jnp.int32),
        ],
        compiler_params=params(),
        cost_estimate=cost(2 * 2 * slots * slots * BLK, 4 * slots * BLK * 2, slots * slots),
        name="attn_forward",
    )(here, chosen, qkv)


def backward_body(
    here_ref,
    chosen_ref,
    qkv_ref,
    grad0,
    grad1,
    grad2,
    grad3,
    attn_ref,
    lse_ref,
    after_ref,
    out_ref,
    q_s,
    k_s,
    v_s,
    g_s,
    kt_s,
    dk_s,
    dv_s,
    grad_ref,
    order_ref,
):
    a, b = here_ref[2], here_ref[3]
    for t, part in enumerate((grad0, grad1, grad2, grad3)):
        grad_ref[t] = part[...]
    live = sort_blocks(chosen_ref, order_ref)
    scale = 1.0 / math.sqrt(BLK)
    scale2 = math.log2(math.e) * scale
    for r in range(NC):
        c = order_ref[r]
        rows = slice(r * BLK, (r + 1) * BLK)

        @pl.when(r // 2 * 2 < live)
        def _():
            k_blk = qkv_ref[c, BLK : 2 * BLK, :]
            q_s[rows, :] = qkv_ref[c, 0:BLK, :]
            k_s[rows, :] = k_blk
            kt_s[:, rows] = k_blk.T
            v_s[rows, :] = qkv_ref[c, 2 * BLK : 3 * BLK, :]
            g_s[rows, :] = grad_ref[b ^ (c % Z), a ^ (c // Z)]

        @pl.when(r >= live)
        def _():
            out_ref[c] = jnp.zeros((3 * BLK, BLK), BF16)

    for p in range(NC // 2):

        @pl.when(2 * p < live)
        def _():
            low = p * PAIR
            q2 = q_s[low : low + PAIR, :]
            g2 = g_s[low : low + PAIR, :]
            deltas = []
            for t in range(2):
                c = order_ref[2 * p + t]
                prod = g2[t * BLK : (t + 1) * BLK, :].astype(F32) * attn_ref[b ^ (c % Z), a ^ (c // Z)].astype(F32)
                deltas.append(jnp.sum(prod.T, axis=0, keepdims=True))
            delta = jnp.concatenate(deltas, axis=1)
            lse = lse_ref[p : p + 1, :]
            dq_t = jnp.zeros((BLK, PAIR), F32)
            for j in range(p + 1):
                keys = slice(j * PAIR, (j + 1) * PAIR)
                s = dot_nt(k_s[keys, :], q2)
                if j == p:
                    s = causal(s)
                prob = jnp.exp2(s * scale2 - lse)
                dprob = dot_nt(v_s[keys, :], g2)
                ds = (prob * (dprob - delta)).astype(BF16)
                dv = dot_nn(prob.astype(BF16), g2)
                dk = dot_nn(ds, q2)
                if j == p:
                    dv_s[keys, :] = dv
                    dk_s[keys, :] = dk
                else:
                    dv_s[keys, :] += dv
                    dk_s[keys, :] += dk
                dq_t = dq_t + dot_nn(kt_s[:, keys], ds)
            dq = (dq_t * scale).T.astype(BF16)
            for t in range(2):
                c = order_ref[2 * p + t]

                @pl.when(2 * p + t < live)
                def _():
                    out_ref[c, 0:BLK, :] = dq[t * BLK : (t + 1) * BLK, :]

    for r in range(NC):
        c = order_ref[r]
        rows = slice(r * BLK, (r + 1) * BLK)

        @pl.when(r < live)
        def _():
            out_ref[c, BLK : 2 * BLK, :] = (dk_s[rows, :] * scale).astype(BF16)
            out_ref[c, 2 * BLK : 3 * BLK, :] = dv_s[rows, :].astype(BF16)


def attn_backward(here, chosen, qkv, grads, attn, lse, after):
    slots = NC * BLK
    return pl.pallas_call(
        backward_body,
        in_specs=[pl.BlockSpec(memory_space=pltpu.SMEM)] * 2 + [pl.BlockSpec(memory_space=pltpu.VMEM)] * 7
        + [pl.BlockSpec(memory_space=pl.ANY)],
        out_shape=jax.ShapeDtypeStruct((NC, 3 * BLK, BLK), BF16),
        scratch_shapes=[
            pltpu.VMEM((slots, BLK), BF16),
            pltpu.VMEM((slots, BLK), BF16),
            pltpu.VMEM((slots, BLK), BF16),
            pltpu.VMEM((slots, BLK), BF16),
            pltpu.VMEM((BLK, slots), BF16),
            pltpu.VMEM((slots, BLK), F32),
            pltpu.VMEM((slots, BLK), F32),
            pltpu.VMEM((Z, Y, BLK, BLK), BF16),
            pltpu.SMEM((NC,), jnp.int32),
        ],
        compiler_params=params(),
        cost_estimate=cost(5 * 2 * slots * slots * BLK, 8 * slots * BLK * 2, slots * slots),
        name="attn_backward",
    )(here, chosen, qkv, *grads, attn, lse, after)


def proj_body(here_ref, *refs):
    attn_refs, wide_ref, g_refs = refs[:Z], refs[Z], refs[Z + 1 : Z + 1 + Y]
    mix_refs, dw_refs = refs[Z + 1 + Y : Z + 1 + 2 * Y], refs[Z + 1 + 2 * Y : Z + 5 + 2 * Y]
    a_s, at_s, g_s = refs[-3:]
    x = here_ref[4]
    for t in range(Z):
        for s in range(Y):
            blk = attn_refs[t][s]
            a_s[s * BLK : (s + 1) * BLK, t * BLK : (t + 1) * BLK] = blk
            at_s[t * BLK : (t + 1) * BLK, s * BLK : (s + 1) * BLK] = blk.T
    for s in range(Y):
        g_s[s * BLK : (s + 1) * BLK, :] = g_refs[s][...]
    width = wide_ref.shape[1] // 4
    for u in range(4):
        cols = pl.ds(pl.multiple_of((x ^ u) * width, width), width)
        for t in range(Z):
            part = dot_nn(at_s[t * BLK : (t + 1) * BLK, :], g_s[:, cols]).astype(BF16)
            for k in range(4):
                dw_refs[u][k, t] = part[:, k * BLK : (k + 1) * BLK]
    for j in range(4):
        cols = slice(j * width, (j + 1) * width)
        for s in range(Y):
            mix_refs[s][:, cols] = dot_nn(a_s[s * BLK : (s + 1) * BLK, :], wide_ref[:, cols]).astype(BF16)


def proj_products(here, attns, wide, grads):
    cols = wide.shape[1]
    vmem = pl.BlockSpec(memory_space=pltpu.VMEM)
    return pl.pallas_call(
        proj_body,
        in_specs=[pl.BlockSpec(memory_space=pltpu.SMEM)] + [vmem] * 9,
        out_shape=[jax.ShapeDtypeStruct((BLK, cols), BF16)] * Y
        + [jax.ShapeDtypeStruct((4, Z, BLK, BLK), BF16)] * 4,
        scratch_shapes=[
            pltpu.VMEM((Y * BLK, Z * BLK), BF16),
            pltpu.VMEM((Z * BLK, Y * BLK), BF16),
            pltpu.VMEM((Y * BLK, cols), BF16),
        ],
        compiler_params=params(),
        cost_estimate=cost(2 * 2 * 512 * 512 * cols, 4 * 512 * cols * 2),
        name="proj_products",
    )(here, *attns, wide, *grads)


def fold_body(count, at, here_ref, *refs):
    ins, outs = refs[:count], refs[count:]
    me = here_ref[at] if at >= 0 else 0
    for v, out in enumerate(outs):
        total = ins[0][me ^ v].astype(F32)
        for i in range(1, count):
            total = total + ins[i][me ^ v].astype(F32)
        out[...] = total.astype(out.dtype)


def fold(here, at, parts, kind):
    shape = parts[0].shape
    vmem = pl.BlockSpec(memory_space=pltpu.VMEM)
    return pl.pallas_call(
        functools.partial(fold_body, len(parts), at),
        in_specs=[pl.BlockSpec(memory_space=pltpu.SMEM)] + [vmem] * len(parts),
        out_shape=[jax.ShapeDtypeStruct(shape[1:], kind)] * shape[0],
        compiler_params=params(),
        cost_estimate=cost(0, 5 * math.prod(shape) * 2),
        name="fold",
    )(here, *parts)


def place_mixed_body(here_ref, chosen_ref, p0, p1, p2, p3, out_ref):
    mine = pl.program_id(0) == half_of(here_ref, chosen_ref)

    @pl.when(mine)
    def _():
        total = p0[...].astype(F32) + p1[...].astype(F32) + p2[...].astype(F32) + p3[...].astype(F32)
        out_ref[0] = total.astype(BF16)

    @pl.when(jnp.logical_not(mine))
    def _():
        out_ref[...] = jnp.zeros(out_ref.shape, BF16)


def place_mixed(here, chosen, parts):
    cols = parts[0].shape[1]
    steps = 2
    width = cols // steps
    return pl.pallas_call(
        place_mixed_body,
        grid_spec=pltpu.PrefetchScalarGridSpec(
            num_scalar_prefetch=2,
            grid=(2, steps),
            in_specs=[pl.BlockSpec((BLK, width), lambda i, j, h, c: (0, j))] * Y,
            out_specs=pl.BlockSpec((1, BLK, width), lambda i, j, h, c: (0, i, j)),
        ),
        out_shape=jax.ShapeDtypeStruct((1, 2 * BLK, cols), BF16),
        compiler_params=params(),
        cost_estimate=cost(0, 6 * BLK * cols * 2),
        name="place_mixed",
    )(here, chosen, *parts)


def place_grads_body(here_ref, chosen_ref, back_ref, q_ref, k_ref, v_ref):
    mine = pl.program_id(0) == half_of(here_ref, chosen_ref)
    heads = back_ref.shape[0]

    @pl.when(mine)
    def _():
        for h in range(heads):
            cols = slice(h * BLK, (h + 1) * BLK)
            for part, out in enumerate((q_ref, k_ref, v_ref)):
                out[0, :, cols] = back_ref[h, part * BLK : (part + 1) * BLK, :]

    @pl.when(jnp.logical_not(mine))
    def _():
        for out in (q_ref, k_ref, v_ref):
            out[...] = jnp.zeros(out.shape, BF16)


def place_grads(here, chosen, back):
    feats = NC * BLK
    steps = 2
    width = feats // steps
    out = pl.BlockSpec((1, BLK, width), lambda i, j, h, c: (0, i, j))
    shape = jax.ShapeDtypeStruct((1, 2 * BLK, feats), BF16)
    return pl.pallas_call(
        place_grads_body,
        grid_spec=pltpu.PrefetchScalarGridSpec(
            num_scalar_prefetch=2,
            grid=(2, steps),
            in_specs=[pl.BlockSpec((NC // steps, 3 * BLK, BLK), lambda i, j, h, c: (j, 0, 0))],
            out_specs=[out] * 3,
        ),
        out_shape=[shape] * 3,
        compiler_params=params(),
        cost_estimate=cost(0, 9 * BLK * feats * 2),
        name="place_grads",
    )(here, chosen, back)


def along_y(x, s):
    return lax.ppermute(x, "ctx", [(c, c ^ (s * Z)) for c in range(NC)])


def along_z(x, t):
    return lax.ppermute(x, "ctx", [(c, c ^ t) for c in range(NC)])


def along_x(x, u):
    return lax.ppermute(x, "dp", [(d, d ^ (u * 4)) for d in range(16)])


def along_k(x, v):
    return lax.ppermute(x, "dp", [(d, d ^ v) for d in range(16)])


def along_chips_z(x, i):
    t, low = i // 2, i % 2
    return lax.ppermute(x, ("dp", "ctx"), [(n, n ^ (low * 2 * NC) ^ t) for n in range(16 * NC)])


def along_core(x):
    return lax.ppermute(x, "dp", [(d, d ^ 1) for d in range(16)])


def spread(x, along):
    return [x] + [along(x, i) for i in (1, 2, 3)]


def swap(parts, along):
    return [parts[0]] + [along(parts[i], i) for i in (1, 2, 3)]


def shards(queries, keys, values, out_grad, chosen, proj):
    picked = chosen[0]
    ctx = lax.axis_index("ctx")
    dp = lax.axis_index("dp")
    here = jnp.stack([ctx, dp, ctx // Z, ctx % Z, dp // 4, dp % 4]).astype(jnp.int32)

    qkv_own, gs = take_rows(here, picked, queries, keys, values, out_grad)

    rows_z = [proj] + [along_chips_z(proj, i) for i in range(1, 8)]
    rows_z, qkv_own = join_rows(rows_z, qkv_own)
    rows_core = jnp.concatenate([rows_z, along_core(rows_z)], 0)
    proj_rows = spread(rows_core, along_x)

    gs_y = spread(gs, along_y)
    qkv = lax.all_to_all(qkv_own, "ctx", 0, 0, tiled=True)

    *grad_parts, wide = attn_grad_product(here, gs_y, proj_rows)
    grads = swap(grad_parts, along_z)

    attn, *attn_parts, lse = attn_forward(here, picked, qkv)
    attns = swap(attn_parts, along_z)
    products = proj_products(here, attns, wide, gs_y)

    back = attn_backward(here, picked, qkv, grads, attn, lse, products[0])
    back = lax.all_to_all(back, "ctx", 0, 0, tiled=True)

    mixed = swap(products[:Y], along_y)
    dw = swap(products[Y:], along_x)
    dw = swap(fold(here, 5, dw, BF16), along_k)
    dw = swap(fold(here, -1, dw, F32), along_z)
    proj_grad = dw[0] + dw[1] + dw[2] + dw[3]

    attn_out = place_mixed(here, picked, mixed)
    q_grad, k_grad, v_grad = place_grads(here, picked, back)
    return attn_out, q_grad, k_grad, v_grad, proj_grad


def solution(mesh):
    rows = P("dp", "ctx", None)
    return jax.shard_map(
        shards,
        mesh=mesh,
        in_specs=(rows, rows, rows, rows, P("dp", None), P("ctx", "dp")),
        out_specs=(rows, rows, rows, rows, P("ctx", "dp")),
        check_vma=False,
    )
```

```python
import functools
import math

import jax
import jax.numpy as jnp
from jax import lax
from jax.experimental import pallas as pl
from jax.experimental.pallas import tpu as pltpu
from jax.sharding import PartitionSpec as P

BLK = 128
Y = 4
Z = 4
NC = Y * Z
PAIR = 2 * BLK
NEG = -1e30
VMEM_BYTES = 48 * 1024 * 1024
F32 = jnp.float32
BF16 = jnp.bfloat16


def dot_nt(a, b):
    return lax.dot_general(a, b, (((1,), (1,)), ((), ())), preferred_element_type=F32)


def dot_nn(a, b):
    return lax.dot_general(a, b, (((1,), (0,)), ((), ())), preferred_element_type=F32)


def params():
    return pltpu.CompilerParams(vmem_limit_bytes=VMEM_BYTES)


def cost(flops, nbytes, trans=0):
    return pl.CostEstimate(flops=flops, bytes_accessed=nbytes, transcendentals=trans)


def half_of(here_ref, chosen_ref):
    pick = chosen_ref[here_ref[0]]
    return ((pick >= 0) & (pick != here_ref[0])).astype(jnp.int32)


def take_body(here_ref, chosen_ref, q_ref, k_ref, v_ref, qkv_ref):
    live = chosen_ref[here_ref[0]] >= 0
    zero = jnp.zeros((), BF16)
    heads = qkv_ref.shape[0]
    for h in range(heads):
        cols = slice(h * BLK, (h + 1) * BLK)
        for part, src in enumerate((q_ref, k_ref, v_ref)):
            qkv_ref[h, part * BLK : (part + 1) * BLK, :] = jnp.where(live, src[0, :, cols], zero)


def take_heads(here, chosen, queries, keys, values):
    feats = queries.shape[2]
    steps = 4
    width = feats // steps
    src = pl.BlockSpec((1, BLK, width), lambda i, h, c: (0, half_of(h, c), i))
    return pl.pallas_call(
        take_body,
        grid_spec=pltpu.PrefetchScalarGridSpec(
            num_scalar_prefetch=2,
            grid=(steps,),
            in_specs=[src] * 3,
            out_specs=pl.BlockSpec((NC // steps, 3 * BLK, BLK), lambda i, h, c: (i, 0, 0)),
        ),
        out_shape=jax.ShapeDtypeStruct((NC, 3 * BLK, BLK), BF16),
        compiler_params=pltpu.CompilerParams(vmem_limit_bytes=62 * 1024 * 1024),
        cost_estimate=cost(0, 6 * BLK * feats * 2),
        name="take_heads",
    )(here, chosen, queries, keys, values)


def take_grad_body(here_ref, chosen_ref, g_ref, gs_ref):
    live = chosen_ref[here_ref[0]] >= 0
    gs_ref[...] = jnp.where(live, g_ref[0], jnp.zeros((), BF16))


def take_grad(here, chosen, out_grad):
    feats = out_grad.shape[2]
    return pl.pallas_call(
        take_grad_body,
        grid_spec=pltpu.PrefetchScalarGridSpec(
            num_scalar_prefetch=2,
            grid=(2,),
            in_specs=[pl.BlockSpec((1, BLK // 2, feats), lambda i, h, c: (0, 2 * half_of(h, c) + i, 0))],
            out_specs=pl.BlockSpec((BLK // 2, feats), lambda i, h, c: (i, 0)),
        ),
        out_shape=jax.ShapeDtypeStruct((BLK, feats), BF16),
        compiler_params=pltpu.CompilerParams(vmem_limit_bytes=62 * 1024 * 1024),
        cost_estimate=cost(0, 2 * BLK * feats * 2),
        name="take_grad",
    )(here, chosen, out_grad)


def attn_grad_body(here_ref, *refs):
    g_refs, w_refs, outs, wide_ref = refs[:Y], refs[Y : 2 * Y], refs[2 * Y : 2 * Y + Z], refs[-1]
    x, k = here_ref[4], here_ref[5]
    for u in range(4):
        for v in range(4):
            d = (x ^ u) * 4 + (k ^ v)
            cols = pl.ds(pl.multiple_of(d * BLK, BLK), BLK)
            for t in range(Z):
                wide_ref[t * BLK : (t + 1) * BLK, cols] = w_refs[u][(v % 2) * 8 + t * 2 + v // 2]
    for t in range(Z):
        for s in range(Y):
            outs[t][s] = dot_nt(g_refs[s][...], wide_ref[t * BLK : (t + 1) * BLK, :]).astype(BF16)


def attn_grad_product(here, grads, proj_rows):
    cols = grads[0].shape[1]
    vmem = pl.BlockSpec(memory_space=pltpu.VMEM)
    return pl.pallas_call(
        attn_grad_body,
        in_specs=[pl.BlockSpec(memory_space=pltpu.SMEM)] + [vmem] * 8,
        out_shape=[jax.ShapeDtypeStruct((Y, BLK, BLK), BF16)] * Z
        + [jax.ShapeDtypeStruct((Z * BLK, cols), BF16)],
        compiler_params=params(),
        cost_estimate=cost(2 * 512 * 512 * cols, 3 * 512 * cols * 2),
        name="attn_grad_product",
    )(here, *grads, *proj_rows)


def sort_blocks(chosen_ref, order_ref):
    count = jnp.int32(0)
    for pos in range(2 * NC):
        c = pos if pos < NC else 2 * NC - 1 - pos
        hit = chosen_ref[c] == pos

        @pl.when(hit)
        def _():
            order_ref[count] = c

        count = count + hit.astype(jnp.int32)
    live = count
    for c in range(NC):
        hit = chosen_ref[c] < 0

        @pl.when(hit)
        def _():
            order_ref[count] = c

        count = count + hit.astype(jnp.int32)
    return live


def causal(s):
    key = lax.broadcasted_iota(jnp.int32, s.shape, 0)
    query = lax.broadcasted_iota(jnp.int32, s.shape, 1)
    return jnp.where(key <= query, s, NEG)


def forward_body(
    here_ref, chosen_ref, qkv_ref, attn_ref, out0, out1, out2, out3, lse_ref, q_s, k_s, vt_s, order_ref
):
    a, b = here_ref[2], here_ref[3]
    live = sort_blocks(chosen_ref, order_ref)
    scale2 = math.log2(math.e) / math.sqrt(BLK)
    for r in range(NC):
        c = order_ref[r]
        rows = slice(r * BLK, (r + 1) * BLK)

        @pl.when(r // 2 * 2 < live)
        def _():
            q_s[rows, :] = qkv_ref[c, 0:BLK, :]
            k_s[rows, :] = qkv_ref[c, BLK : 2 * BLK, :]
            vt_s[:, rows] = qkv_ref[c, 2 * BLK : 3 * BLK, :].T

        @pl.when(r >= live)
        def _():
            attn_ref[b ^ (c % Z), a ^ (c // Z)] = jnp.zeros((BLK, BLK), BF16)

    for p in range(NC // 2):

        @pl.when(2 * p < live)
        def _():
            low = p * PAIR
            q2 = q_s[low : low + PAIR, :]
            diag = causal(dot_nt(k_s[low : low + PAIR, :], q2))
            parts = [(low, diag)]
            top = jnp.max(diag, axis=0, keepdims=True)
            for j in range(p):
                s = dot_nt(k_s[j * PAIR : (j + 1) * PAIR, :], q2)
                top = jnp.maximum(top, jnp.max(s, axis=0, keepdims=True))
                parts.append((j * PAIR, s))
            total = jnp.zeros((1, PAIR), F32)
            out_t = jnp.zeros((BLK, PAIR), F32)
            shift = top * scale2
            for start, s in parts:
                e = jnp.exp2(s * scale2 - shift)
                total = total + jnp.sum(e, axis=0, keepdims=True)
                out_t = out_t + dot_nn(vt_s[:, start : start + PAIR], e.astype(BF16))
            lse_ref[p : p + 1, :] = shift + jnp.log2(total)
            out = (out_t * (1.0 / total)).T.astype(BF16)
            for t in range(2):
                c = order_ref[2 * p + t]

                @pl.when(2 * p + t < live)
                def _():
                    attn_ref[b ^ (c % Z), a ^ (c // Z)] = out[t * BLK : (t + 1) * BLK, :]

    for t, out_ref in enumerate((out0, out1, out2, out3)):
        out_ref[...] = attn_ref[t]


def attn_forward(here, chosen, qkv):
    slots = NC * BLK
    return pl.pallas_call(
        forward_body,
        in_specs=[
            pl.BlockSpec(memory_space=pltpu.SMEM),
            pl.BlockSpec(memory_space=pltpu.SMEM),
            pl.BlockSpec(memory_space=pltpu.VMEM),
        ],
        out_shape=[jax.ShapeDtypeStruct((Z, Y, BLK, BLK), BF16)]
        + [jax.ShapeDtypeStruct((Y, BLK, BLK), BF16)] * Z
        + [
            jax.ShapeDtypeStruct((NC // 2, PAIR), F32),
        ],
        scratch_shapes=[
            pltpu.VMEM((slots, BLK), BF16),
            pltpu.VMEM((slots, BLK), BF16),
            pltpu.VMEM((BLK, slots), BF16),
            pltpu.SMEM((NC,), jnp.int32),
        ],
        compiler_params=params(),
        cost_estimate=cost(2 * 2 * slots * slots * BLK, 4 * slots * BLK * 2, slots * slots),
        name="attn_forward",
    )(here, chosen, qkv)


def backward_body(
    here_ref,
    chosen_ref,
    qkv_ref,
    grad0,
    grad1,
    grad2,
    grad3,
    attn_ref,
    lse_ref,
    out_ref,
    q_s,
    k_s,
    v_s,
    g_s,
    kt_s,
    dk_s,
    dv_s,
    grad_ref,
    order_ref,
):
    a, b = here_ref[2], here_ref[3]
    for t, part in enumerate((grad0, grad1, grad2, grad3)):
        grad_ref[t] = part[...]
    live = sort_blocks(chosen_ref, order_ref)
    scale = 1.0 / math.sqrt(BLK)
    scale2 = math.log2(math.e) * scale
    for r in range(NC):
        c = order_ref[r]
        rows = slice(r * BLK, (r + 1) * BLK)

        @pl.when(r // 2 * 2 < live)
        def _():
            k_blk = qkv_ref[c, BLK : 2 * BLK, :]
            q_s[rows, :] = qkv_ref[c, 0:BLK, :]
            k_s[rows, :] = k_blk
            kt_s[:, rows] = k_blk.T
            v_s[rows, :] = qkv_ref[c, 2 * BLK : 3 * BLK, :]
            g_s[rows, :] = grad_ref[b ^ (c % Z), a ^ (c // Z)]

        @pl.when(r >= live)
        def _():
            out_ref[c] = jnp.zeros((3 * BLK, BLK), BF16)

    for p in range(NC // 2):

        @pl.when(2 * p < live)
        def _():
            low = p * PAIR
            q2 = q_s[low : low + PAIR, :]
            g2 = g_s[low : low + PAIR, :]
            deltas = []
            for t in range(2):
                c = order_ref[2 * p + t]
                prod = g2[t * BLK : (t + 1) * BLK, :].astype(F32) * attn_ref[b ^ (c % Z), a ^ (c // Z)].astype(F32)
                deltas.append(jnp.sum(prod.T, axis=0, keepdims=True))
            delta = jnp.concatenate(deltas, axis=1)
            lse = lse_ref[p : p + 1, :]
            dq_t = jnp.zeros((BLK, PAIR), F32)
            for j in range(p + 1):
                keys = slice(j * PAIR, (j + 1) * PAIR)
                s = dot_nt(k_s[keys, :], q2)
                if j == p:
                    s = causal(s)
                prob = jnp.exp2(s * scale2 - lse)
                dprob = dot_nt(v_s[keys, :], g2)
                ds = (prob * (dprob - delta)).astype(BF16)
                dv = dot_nn(prob.astype(BF16), g2)
                dk = dot_nn(ds, q2)
                if j == p:
                    dv_s[keys, :] = dv
                    dk_s[keys, :] = dk
                else:
                    dv_s[keys, :] += dv
                    dk_s[keys, :] += dk
                dq_t = dq_t + dot_nn(kt_s[:, keys], ds)
            dq = (dq_t * scale).T.astype(BF16)
            for t in range(2):
                c = order_ref[2 * p + t]

                @pl.when(2 * p + t < live)
                def _():
                    out_ref[c, 0:BLK, :] = dq[t * BLK : (t + 1) * BLK, :]

    for r in range(NC):
        c = order_ref[r]
        rows = slice(r * BLK, (r + 1) * BLK)

        @pl.when(r < live)
        def _():
            out_ref[c, BLK : 2 * BLK, :] = (dk_s[rows, :] * scale).astype(BF16)
            out_ref[c, 2 * BLK : 3 * BLK, :] = dv_s[rows, :].astype(BF16)


def attn_backward(here, chosen, qkv, grads, attn, lse):
    slots = NC * BLK
    return pl.pallas_call(
        backward_body,
        in_specs=[pl.BlockSpec(memory_space=pltpu.SMEM)] * 2 + [pl.BlockSpec(memory_space=pltpu.VMEM)] * 7,
        out_shape=jax.ShapeDtypeStruct((NC, 3 * BLK, BLK), BF16),
        scratch_shapes=[
            pltpu.VMEM((slots, BLK), BF16),
            pltpu.VMEM((slots, BLK), BF16),
            pltpu.VMEM((slots, BLK), BF16),
            pltpu.VMEM((slots, BLK), BF16),
            pltpu.VMEM((BLK, slots), BF16),
            pltpu.VMEM((slots, BLK), F32),
            pltpu.VMEM((slots, BLK), F32),
            pltpu.VMEM((Z, Y, BLK, BLK), BF16),
            pltpu.SMEM((NC,), jnp.int32),
        ],
        compiler_params=params(),
        cost_estimate=cost(5 * 2 * slots * slots * BLK, 8 * slots * BLK * 2, slots * slots),
        name="attn_backward",
    )(here, chosen, qkv, *grads, attn, lse)


def proj_body(here_ref, *refs):
    attn_refs, wide_ref, g_refs = refs[:Z], refs[Z], refs[Z + 1 : Z + 1 + Y]
    mix_refs, dw_refs = refs[Z + 1 + Y : Z + 1 + 2 * Y], refs[Z + 1 + 2 * Y : Z + 5 + 2 * Y]
    a_s, at_s, g_s = refs[-3:]
    x = here_ref[4]
    for t in range(Z):
        for s in range(Y):
            blk = attn_refs[t][s]
            a_s[s * BLK : (s + 1) * BLK, t * BLK : (t + 1) * BLK] = blk
            at_s[t * BLK : (t + 1) * BLK, s * BLK : (s + 1) * BLK] = blk.T
    for s in range(Y):
        g_s[s * BLK : (s + 1) * BLK, :] = g_refs[s][...]
    width = wide_ref.shape[1] // 4
    for u in range(4):
        cols = pl.ds(pl.multiple_of((x ^ u) * width, width), width)
        for t in range(Z):
            part = dot_nn(at_s[t * BLK : (t + 1) * BLK, :], g_s[:, cols]).astype(BF16)
            for k in range(4):
                dw_refs[u][k, t] = part[:, k * BLK : (k + 1) * BLK]
    for j in range(4):
        cols = slice(j * width, (j + 1) * width)
        for s in range(Y):
            mix_refs[s][:, cols] = dot_nn(a_s[s * BLK : (s + 1) * BLK, :], wide_ref[:, cols]).astype(BF16)


def proj_products(here, attns, wide, grads):
    cols = wide.shape[1]
    vmem = pl.BlockSpec(memory_space=pltpu.VMEM)
    return pl.pallas_call(
        proj_body,
        in_specs=[pl.BlockSpec(memory_space=pltpu.SMEM)] + [vmem] * 9,
        out_shape=[jax.ShapeDtypeStruct((BLK, cols), BF16)] * Y
        + [jax.ShapeDtypeStruct((4, Z, BLK, BLK), BF16)] * 4,
        scratch_shapes=[
            pltpu.VMEM((Y * BLK, Z * BLK), BF16),
            pltpu.VMEM((Z * BLK, Y * BLK), BF16),
            pltpu.VMEM((Y * BLK, cols), BF16),
        ],
        compiler_params=params(),
        cost_estimate=cost(2 * 2 * 512 * 512 * cols, 4 * 512 * cols * 2),
        name="proj_products",
    )(here, *attns, wide, *grads)


def fold_body(count, at, here_ref, *refs):
    ins, outs = refs[:count], refs[count:]
    me = here_ref[at] if at >= 0 else 0
    for v, out in enumerate(outs):
        total = ins[0][me ^ v].astype(F32)
        for i in range(1, count):
            total = total + ins[i][me ^ v].astype(F32)
        out[...] = total.astype(out.dtype)


def fold(here, at, parts, kind):
    shape = parts[0].shape
    vmem = pl.BlockSpec(memory_space=pltpu.VMEM)
    return pl.pallas_call(
        functools.partial(fold_body, len(parts), at),
        in_specs=[pl.BlockSpec(memory_space=pltpu.SMEM)] + [vmem] * len(parts),
        out_shape=[jax.ShapeDtypeStruct(shape[1:], kind)] * shape[0],
        compiler_params=params(),
        cost_estimate=cost(0, 5 * math.prod(shape) * 2),
        name="fold",
    )(here, *parts)


def place_mixed_body(here_ref, chosen_ref, p0, p1, p2, p3, out_ref):
    mine = pl.program_id(0) == half_of(here_ref, chosen_ref)

    @pl.when(mine)
    def _():
        total = p0[...].astype(F32) + p1[...].astype(F32) + p2[...].astype(F32) + p3[...].astype(F32)
        out_ref[0] = total.astype(BF16)

    @pl.when(jnp.logical_not(mine))
    def _():
        out_ref[...] = jnp.zeros(out_ref.shape, BF16)


def place_mixed(here, chosen, parts):
    cols = parts[0].shape[1]
    steps = 2
    width = cols // steps
    return pl.pallas_call(
        place_mixed_body,
        grid_spec=pltpu.PrefetchScalarGridSpec(
            num_scalar_prefetch=2,
            grid=(2, steps),
            in_specs=[pl.BlockSpec((BLK, width), lambda i, j, h, c: (0, j))] * Y,
            out_specs=pl.BlockSpec((1, BLK, width), lambda i, j, h, c: (0, i, j)),
        ),
        out_shape=jax.ShapeDtypeStruct((1, 2 * BLK, cols), BF16),
        compiler_params=params(),
        cost_estimate=cost(0, 6 * BLK * cols * 2),
        name="place_mixed",
    )(here, chosen, *parts)


def place_grads_body(here_ref, chosen_ref, back_ref, q_ref, k_ref, v_ref):
    mine = pl.program_id(0) == half_of(here_ref, chosen_ref)
    heads = back_ref.shape[0]

    @pl.when(mine)
    def _():
        for h in range(heads):
            cols = slice(h * BLK, (h + 1) * BLK)
            for part, out in enumerate((q_ref, k_ref, v_ref)):
                out[0, :, cols] = back_ref[h, part * BLK : (part + 1) * BLK, :]

    @pl.when(jnp.logical_not(mine))
    def _():
        for out in (q_ref, k_ref, v_ref):
            out[...] = jnp.zeros(out.shape, BF16)


def place_grads(here, chosen, back):
    feats = NC * BLK
    steps = 2
    width = feats // steps
    out = pl.BlockSpec((1, BLK, width), lambda i, j, h, c: (0, i, j))
    shape = jax.ShapeDtypeStruct((1, 2 * BLK, feats), BF16)
    return pl.pallas_call(
        place_grads_body,
        grid_spec=pltpu.PrefetchScalarGridSpec(
            num_scalar_prefetch=2,
            grid=(2, steps),
            in_specs=[pl.BlockSpec((NC // steps, 3 * BLK, BLK), lambda i, j, h, c: (j, 0, 0))],
            out_specs=[out] * 3,
        ),
        out_shape=[shape] * 3,
        compiler_params=params(),
        cost_estimate=cost(0, 9 * BLK * feats * 2),
        name="place_grads",
    )(here, chosen, back)


def along_y(x, s):
    return lax.ppermute(x, "ctx", [(c, c ^ (s * Z)) for c in range(NC)])


def along_z(x, t):
    return lax.ppermute(x, "ctx", [(c, c ^ t) for c in range(NC)])


def along_x(x, u):
    return lax.ppermute(x, "dp", [(d, d ^ (u * 4)) for d in range(16)])


def along_k(x, v):
    return lax.ppermute(x, "dp", [(d, d ^ v) for d in range(16)])


def along_z_lo(x):
    return lax.ppermute(x, "dp", [(d, d ^ 2) for d in range(16)])


def along_core(x):
    return lax.ppermute(x, "dp", [(d, d ^ 1) for d in range(16)])


def spread(x, along):
    return [x] + [along(x, i) for i in (1, 2, 3)]


def swap(parts, along):
    return [parts[0]] + [along(parts[i], i) for i in (1, 2, 3)]


def shards(queries, keys, values, out_grad, chosen, proj):
    picked = chosen[0]
    ctx = lax.axis_index("ctx")
    dp = lax.axis_index("dp")
    here = jnp.stack([ctx, dp, ctx // Z, ctx % Z, dp // 4, dp % 4]).astype(jnp.int32)

    gs = take_grad(here, picked, out_grad)
    gs_y = spread(gs, along_y)
    qkv_own = take_heads(here, picked, queries, keys, values)

    rows_low = jnp.stack([proj, along_z_lo(proj)])
    rows_z, gs_y[1], gs_y[3], qkv_own = lax.optimization_barrier(
        (spread(rows_low, along_z), gs_y[1], gs_y[3], qkv_own)
    )
    rows_z = jnp.concatenate(rows_z, 0)
    rows_core = jnp.concatenate([rows_z, along_core(rows_z)], 0)
    proj_rows = spread(rows_core, along_x)

    qkv = lax.all_to_all(qkv_own, "ctx", 0, 0, tiled=True)

    *grad_parts, wide = attn_grad_product(here, gs_y, proj_rows)
    qkv, grad_parts = lax.optimization_barrier((qkv, grad_parts))
    grads = swap(grad_parts, along_z)

    attn, *attn_parts, lse = attn_forward(here, picked, qkv)
    attns = swap(attn_parts, along_z)

    back = attn_backward(here, picked, qkv, grads, attn, lse)
    back, attns = lax.optimization_barrier((back, attns))
    back = lax.all_to_all(back, "ctx", 0, 0, tiled=True)

    products = proj_products(here, attns, wide, gs_y)
    mixed = swap(products[:Y], along_y)
    dw = swap(products[Y:], along_x)
    dw = swap(fold(here, 5, dw, BF16), along_k)
    dw = swap(fold(here, -1, dw, F32), along_z)
    proj_grad = dw[0] + dw[1] + dw[2] + dw[3]

    attn_out = place_mixed(here, picked, mixed)
    q_grad, k_grad, v_grad = place_grads(here, picked, back)
    return attn_out, q_grad, k_grad, v_grad, proj_grad


def solution(mesh):
    rows = P("dp", "ctx", None)
    return jax.shard_map(
        shards,
        mesh=mesh,
        in_specs=(rows, rows, rows, rows, P("dp", None), P("ctx", "dp")),
        out_specs=(rows, rows, rows, rows, P("ctx", "dp")),
        check_vma=False,
    )
```

```python
import functools
import math

import jax
import jax.numpy as jnp
from jax import lax
from jax.experimental import pallas as pl
from jax.experimental.pallas import tpu as pltpu
from jax.sharding import PartitionSpec as P

BLK = 128
Y = 4
Z = 4
NC = Y * Z
PAIR = 2 * BLK
NEG = -1e30
VMEM_BYTES = 48 * 1024 * 1024
F32 = jnp.float32
BF16 = jnp.bfloat16


def dot_nt(a, b):
    return lax.dot_general(a, b, (((1,), (1,)), ((), ())), preferred_element_type=F32)


def dot_nn(a, b):
    return lax.dot_general(a, b, (((1,), (0,)), ((), ())), preferred_element_type=F32)


def params():
    return pltpu.CompilerParams(vmem_limit_bytes=VMEM_BYTES)


def cost(flops, nbytes, trans=0):
    return pl.CostEstimate(flops=flops, bytes_accessed=nbytes, transcendentals=trans)


def half_of(here_ref, chosen_ref):
    pick = chosen_ref[here_ref[0]]
    return ((pick >= 0) & (pick != here_ref[0])).astype(jnp.int32)


def take_body(here_ref, chosen_ref, q_ref, k_ref, v_ref, qkv_ref):
    live = chosen_ref[here_ref[0]] >= 0
    zero = jnp.zeros((), BF16)
    heads = qkv_ref.shape[0]
    for h in range(heads):
        cols = slice(h * BLK, (h + 1) * BLK)
        for part, src in enumerate((q_ref, k_ref, v_ref)):
            qkv_ref[h, part * BLK : (part + 1) * BLK, :] = jnp.where(live, src[0, :, cols], zero)


def take_heads(here, chosen, queries, keys, values):
    feats = queries.shape[2]
    steps = 2
    width = feats // steps
    src = pl.BlockSpec((1, BLK, width), lambda i, h, c: (0, half_of(h, c), i))
    return pl.pallas_call(
        take_body,
        grid_spec=pltpu.PrefetchScalarGridSpec(
            num_scalar_prefetch=2,
            grid=(steps,),
            in_specs=[src] * 3,
            out_specs=pl.BlockSpec((NC // steps, 3 * BLK, BLK), lambda i, h, c: (i, 0, 0)),
        ),
        out_shape=jax.ShapeDtypeStruct((NC, 3 * BLK, BLK), BF16),
        compiler_params=pltpu.CompilerParams(vmem_limit_bytes=62 * 1024 * 1024),
        cost_estimate=cost(0, 6 * BLK * feats * 2),
        name="take_heads",
    )(here, chosen, queries, keys, values)


def take_grad_body(here_ref, chosen_ref, g_ref, gs_ref):
    live = chosen_ref[here_ref[0]] >= 0
    gs_ref[...] = jnp.where(live, g_ref[0], jnp.zeros((), BF16))


def take_grad(here, chosen, out_grad):
    feats = out_grad.shape[2]
    return pl.pallas_call(
        take_grad_body,
        grid_spec=pltpu.PrefetchScalarGridSpec(
            num_scalar_prefetch=2,
            grid=(2,),
            in_specs=[pl.BlockSpec((1, BLK // 2, feats), lambda i, h, c: (0, 2 * half_of(h, c) + i, 0))],
            out_specs=pl.BlockSpec((BLK // 2, feats), lambda i, h, c: (i, 0)),
        ),
        out_shape=jax.ShapeDtypeStruct((BLK, feats), BF16),
        compiler_params=pltpu.CompilerParams(vmem_limit_bytes=62 * 1024 * 1024),
        cost_estimate=cost(0, 2 * BLK * feats * 2),
        name="take_grad",
    )(here, chosen, out_grad)


def attn_grad_body(here_ref, *refs):
    g_refs, w_refs, outs, wide_ref = refs[:Y], refs[Y : Y + 8], refs[Y + 8 : Y + 8 + Z], refs[-1]
    x, k = here_ref[4], here_ref[5]
    for u in range(4):
        for v in range(4):
            d = (x ^ u) * 4 + (k ^ v)
            cols = pl.ds(pl.multiple_of(d * BLK, BLK), BLK)
            for t in range(Z):
                wide_ref[t * BLK : (t + 1) * BLK, cols] = w_refs[4 * (v % 2) + u][t * 2 + v // 2]
    for t in range(Z):
        for s in range(Y):
            outs[t][s] = dot_nt(g_refs[s][...], wide_ref[t * BLK : (t + 1) * BLK, :]).astype(BF16)


def attn_grad_product(here, grads, proj_rows):
    cols = grads[0].shape[1]
    vmem = pl.BlockSpec(memory_space=pltpu.VMEM)
    return pl.pallas_call(
        attn_grad_body,
        in_specs=[pl.BlockSpec(memory_space=pltpu.SMEM)] + [vmem] * (Y + 8),
        out_shape=[jax.ShapeDtypeStruct((Y, BLK, BLK), BF16)] * Z
        + [jax.ShapeDtypeStruct((Z * BLK, cols), BF16)],
        compiler_params=params(),
        cost_estimate=cost(2 * 512 * 512 * cols, 3 * 512 * cols * 2),
        name="attn_grad_product",
    )(here, *grads, *proj_rows)


def sort_blocks(chosen_ref, order_ref):
    count = jnp.int32(0)
    for pos in range(2 * NC):
        c = pos if pos < NC else 2 * NC - 1 - pos
        hit = chosen_ref[c] == pos

        @pl.when(hit)
        def _():
            order_ref[count] = c

        count = count + hit.astype(jnp.int32)
    live = count
    for c in range(NC):
        hit = chosen_ref[c] < 0

        @pl.when(hit)
        def _():
            order_ref[count] = c

        count = count + hit.astype(jnp.int32)
    return live


def causal(s):
    key = lax.broadcasted_iota(jnp.int32, s.shape, 0)
    query = lax.broadcasted_iota(jnp.int32, s.shape, 1)
    return jnp.where(key <= query, s, NEG)


def forward_body(
    here_ref, chosen_ref, qkv_ref, attn_ref, out0, out1, out2, out3, lse_ref, q_s, k_s, vt_s, order_ref
):
    a, b = here_ref[2], here_ref[3]
    live = sort_blocks(chosen_ref, order_ref)
    scale2 = math.log2(math.e) / math.sqrt(BLK)
    for r in range(NC):
        c = order_ref[r]
        rows = slice(r * BLK, (r + 1) * BLK)

        @pl.when(r // 2 * 2 < live)
        def _():
            q_s[rows, :] = qkv_ref[c, 0:BLK, :]
            k_s[rows, :] = qkv_ref[c, BLK : 2 * BLK, :]
            vt_s[:, rows] = qkv_ref[c, 2 * BLK : 3 * BLK, :].T

        @pl.when(r >= live)
        def _():
            attn_ref[b ^ (c % Z), a ^ (c // Z)] = jnp.zeros((BLK, BLK), BF16)

    for p in range(NC // 2):

        @pl.when(2 * p < live)
        def _():
            low = p * PAIR
            q2 = q_s[low : low + PAIR, :]
            diag = causal(dot_nt(k_s[low : low + PAIR, :], q2))
            parts = [(low, diag)]
            top = jnp.max(diag, axis=0, keepdims=True)
            for j in range(p):
                s = dot_nt(k_s[j * PAIR : (j + 1) * PAIR, :], q2)
                top = jnp.maximum(top, jnp.max(s, axis=0, keepdims=True))
                parts.append((j * PAIR, s))
            total = jnp.zeros((1, PAIR), F32)
            out_t = jnp.zeros((BLK, PAIR), F32)
            shift = top * scale2
            for start, s in parts:
                e = jnp.exp2(s * scale2 - shift)
                total = total + jnp.sum(e, axis=0, keepdims=True)
                out_t = out_t + dot_nn(vt_s[:, start : start + PAIR], e.astype(BF16))
            lse_ref[p : p + 1, :] = shift + jnp.log2(total)
            out = (out_t * (1.0 / total)).T.astype(BF16)
            for t in range(2):
                c = order_ref[2 * p + t]

                @pl.when(2 * p + t < live)
                def _():
                    attn_ref[b ^ (c % Z), a ^ (c // Z)] = out[t * BLK : (t + 1) * BLK, :]

    for t, out_ref in enumerate((out0, out1, out2, out3)):
        out_ref[...] = attn_ref[t]


def attn_forward(here, chosen, qkv):
    slots = NC * BLK
    return pl.pallas_call(
        forward_body,
        in_specs=[
            pl.BlockSpec(memory_space=pltpu.SMEM),
            pl.BlockSpec(memory_space=pltpu.SMEM),
            pl.BlockSpec(memory_space=pltpu.VMEM),
        ],
        out_shape=[jax.ShapeDtypeStruct((Z, Y, BLK, BLK), BF16)]
        + [jax.ShapeDtypeStruct((Y, BLK, BLK), BF16)] * Z
        + [
            jax.ShapeDtypeStruct((NC // 2, PAIR), F32),
        ],
        scratch_shapes=[
            pltpu.VMEM((slots, BLK), BF16),
            pltpu.VMEM((slots, BLK), BF16),
            pltpu.VMEM((BLK, slots), BF16),
            pltpu.SMEM((NC,), jnp.int32),
        ],
        compiler_params=params(),
        cost_estimate=cost(2 * 2 * slots * slots * BLK, 4 * slots * BLK * 2, slots * slots),
        name="attn_forward",
    )(here, chosen, qkv)


def backward_body(
    here_ref,
    chosen_ref,
    qkv_ref,
    grad0,
    grad1,
    grad2,
    grad3,
    attn_ref,
    lse_ref,
    out_ref,
    q_s,
    k_s,
    v_s,
    g_s,
    kt_s,
    dk_s,
    dv_s,
    grad_ref,
    order_ref,
):
    a, b = here_ref[2], here_ref[3]
    for t, part in enumerate((grad0, grad1, grad2, grad3)):
        grad_ref[t] = part[...]
    live = sort_blocks(chosen_ref, order_ref)
    scale = 1.0 / math.sqrt(BLK)
    scale2 = math.log2(math.e) * scale
    for r in range(NC):
        c = order_ref[r]
        rows = slice(r * BLK, (r + 1) * BLK)

        @pl.when(r // 2 * 2 < live)
        def _():
            k_blk = qkv_ref[c, BLK : 2 * BLK, :]
            q_s[rows, :] = qkv_ref[c, 0:BLK, :]
            k_s[rows, :] = k_blk
            kt_s[:, rows] = k_blk.T
            v_s[rows, :] = qkv_ref[c, 2 * BLK : 3 * BLK, :]
            g_s[rows, :] = grad_ref[b ^ (c % Z), a ^ (c // Z)]

        @pl.when(r >= live)
        def _():
            out_ref[c] = jnp.zeros((3 * BLK, BLK), BF16)

    for p in range(NC // 2):

        @pl.when(2 * p < live)
        def _():
            low = p * PAIR
            q2 = q_s[low : low + PAIR, :]
            g2 = g_s[low : low + PAIR, :]
            deltas = []
            for t in range(2):
                c = order_ref[2 * p + t]
                prod = g2[t * BLK : (t + 1) * BLK, :].astype(F32) * attn_ref[b ^ (c % Z), a ^ (c // Z)].astype(F32)
                deltas.append(jnp.sum(prod.T, axis=0, keepdims=True))
            delta = jnp.concatenate(deltas, axis=1)
            lse = lse_ref[p : p + 1, :]
            dq_t = jnp.zeros((BLK, PAIR), F32)
            for j in range(p + 1):
                keys = slice(j * PAIR, (j + 1) * PAIR)
                s = dot_nt(k_s[keys, :], q2)
                if j == p:
                    s = causal(s)
                prob = jnp.exp2(s * scale2 - lse)
                dprob = dot_nt(v_s[keys, :], g2)
                ds = (prob * (dprob - delta)).astype(BF16)
                dv = dot_nn(prob.astype(BF16), g2)
                dk = dot_nn(ds, q2)
                if j == p:
                    dv_s[keys, :] = dv
                    dk_s[keys, :] = dk
                else:
                    dv_s[keys, :] += dv
                    dk_s[keys, :] += dk
                dq_t = dq_t + dot_nn(kt_s[:, keys], ds)
            dq = (dq_t * scale).T.astype(BF16)
            for t in range(2):
                c = order_ref[2 * p + t]

                @pl.when(2 * p + t < live)
                def _():
                    out_ref[c, 0:BLK, :] = dq[t * BLK : (t + 1) * BLK, :]

    for r in range(NC):
        c = order_ref[r]
        rows = slice(r * BLK, (r + 1) * BLK)

        @pl.when(r < live)
        def _():
            out_ref[c, BLK : 2 * BLK, :] = (dk_s[rows, :] * scale).astype(BF16)
            out_ref[c, 2 * BLK : 3 * BLK, :] = dv_s[rows, :].astype(BF16)


def attn_backward(here, chosen, qkv, grads, attn, lse):
    slots = NC * BLK
    return pl.pallas_call(
        backward_body,
        in_specs=[pl.BlockSpec(memory_space=pltpu.SMEM)] * 2 + [pl.BlockSpec(memory_space=pltpu.VMEM)] * 7,
        out_shape=jax.ShapeDtypeStruct((NC, 3 * BLK, BLK), BF16),
        scratch_shapes=[
            pltpu.VMEM((slots, BLK), BF16),
            pltpu.VMEM((slots, BLK), BF16),
            pltpu.VMEM((slots, BLK), BF16),
            pltpu.VMEM((slots, BLK), BF16),
            pltpu.VMEM((BLK, slots), BF16),
            pltpu.VMEM((slots, BLK), F32),
            pltpu.VMEM((slots, BLK), F32),
            pltpu.VMEM((Z, Y, BLK, BLK), BF16),
            pltpu.SMEM((NC,), jnp.int32),
        ],
        compiler_params=params(),
        cost_estimate=cost(5 * 2 * slots * slots * BLK, 8 * slots * BLK * 2, slots * slots),
        name="attn_backward",
    )(here, chosen, qkv, *grads, attn, lse)


def proj_body(here_ref, *refs):
    attn_refs, wide_ref, g_refs = refs[:Z], refs[Z], refs[Z + 1 : Z + 1 + Y]
    mix_refs, dw_refs = refs[Z + 1 + Y : Z + 1 + 2 * Y], refs[Z + 1 + 2 * Y : Z + 3 + 2 * Y]
    a_s, at_s, g_s, dw_s = refs[-4:]
    x, k = here_ref[4], here_ref[5]
    for t in range(Z):
        for s in range(Y):
            blk = attn_refs[t][s]
            a_s[s * BLK : (s + 1) * BLK, t * BLK : (t + 1) * BLK] = blk
            at_s[t * BLK : (t + 1) * BLK, s * BLK : (s + 1) * BLK] = blk.T
    for s in range(Y):
        g_s[s * BLK : (s + 1) * BLK, :] = g_refs[s][...]
    width = wide_ref.shape[1] // 4
    for u in range(4):
        cols = pl.ds(pl.multiple_of((x ^ u) * width, width), width)
        for t in range(Z):
            part = dot_nn(at_s[t * BLK : (t + 1) * BLK, :], g_s[:, cols]).astype(BF16)
            for j in range(4):
                dw_s[u, j, t] = part[:, j * BLK : (j + 1) * BLK]
    for core, dw_ref in enumerate(dw_refs):
        for low in range(2):
            dw_ref[:, low] = dw_s[:, k ^ (2 * low + core)]
    for j in range(4):
        cols = slice(j * width, (j + 1) * width)
        for s in range(Y):
            mix_refs[s][:, cols] = dot_nn(a_s[s * BLK : (s + 1) * BLK, :], wide_ref[:, cols]).astype(BF16)


def proj_products(here, attns, wide, grads):
    cols = wide.shape[1]
    vmem = pl.BlockSpec(memory_space=pltpu.VMEM)
    return pl.pallas_call(
        proj_body,
        in_specs=[pl.BlockSpec(memory_space=pltpu.SMEM)] + [vmem] * 9,
        out_shape=[jax.ShapeDtypeStruct((BLK, cols), BF16)] * Y
        + [jax.ShapeDtypeStruct((4, 2, Z, BLK, BLK), BF16)] * 2,
        scratch_shapes=[
            pltpu.VMEM((Y * BLK, Z * BLK), BF16),
            pltpu.VMEM((Z * BLK, Y * BLK), BF16),
            pltpu.VMEM((Y * BLK, cols), BF16),
            pltpu.VMEM((4, 4, Z, BLK, BLK), BF16),
        ],
        compiler_params=params(),
        cost_estimate=cost(2 * 2 * 512 * 512 * cols, 4 * 512 * cols * 2),
        name="proj_products",
    )(here, *attns, wide, *grads)


def fold_body(count, *refs):
    ins, outs = refs[:count], refs[count:]
    for i, out in enumerate(outs):
        total = ins[0][i].astype(F32)
        for part in ins[1:]:
            total = total + part[i].astype(F32)
        out[...] = total.astype(out.dtype)


def fold(parts, kind):
    shape = parts[0].shape
    return pl.pallas_call(
        functools.partial(fold_body, len(parts)),
        out_shape=[jax.ShapeDtypeStruct(shape[1:], kind)] * shape[0],
        compiler_params=params(),
        cost_estimate=cost(0, 5 * math.prod(shape) * 2),
        name="fold",
    )(*parts)


def place_mixed_body(here_ref, chosen_ref, p0, p1, p2, p3, out_ref):
    mine = pl.program_id(0) == half_of(here_ref, chosen_ref)

    @pl.when(mine)
    def _():
        total = p0[...].astype(F32) + p1[...].astype(F32) + p2[...].astype(F32) + p3[...].astype(F32)
        out_ref[0] = total.astype(BF16)

    @pl.when(jnp.logical_not(mine))
    def _():
        out_ref[...] = jnp.zeros(out_ref.shape, BF16)


def place_mixed(here, chosen, parts):
    cols = parts[0].shape[1]
    steps = 2
    width = cols // steps
    return pl.pallas_call(
        place_mixed_body,
        grid_spec=pltpu.PrefetchScalarGridSpec(
            num_scalar_prefetch=2,
            grid=(2, steps),
            in_specs=[pl.BlockSpec((BLK, width), lambda i, j, h, c: (0, j))] * Y,
            out_specs=pl.BlockSpec((1, BLK, width), lambda i, j, h, c: (0, i, j)),
        ),
        out_shape=jax.ShapeDtypeStruct((1, 2 * BLK, cols), BF16),
        compiler_params=params(),
        cost_estimate=cost(0, 6 * BLK * cols * 2),
        name="place_mixed",
    )(here, chosen, *parts)


def place_grads_body(here_ref, chosen_ref, back_ref, q_ref, k_ref, v_ref):
    mine = pl.program_id(0) == half_of(here_ref, chosen_ref)
    heads = back_ref.shape[0]

    @pl.when(mine)
    def _():
        for h in range(heads):
            cols = slice(h * BLK, (h + 1) * BLK)
            for part, out in enumerate((q_ref, k_ref, v_ref)):
                out[0, :, cols] = back_ref[h, part * BLK : (part + 1) * BLK, :]

    @pl.when(jnp.logical_not(mine))
    def _():
        for out in (q_ref, k_ref, v_ref):
            out[...] = jnp.zeros(out.shape, BF16)


def place_grads(here, chosen, back):
    feats = NC * BLK
    steps = 2
    width = feats // steps
    out = pl.BlockSpec((1, BLK, width), lambda i, j, h, c: (0, i, j))
    shape = jax.ShapeDtypeStruct((1, 2 * BLK, feats), BF16)
    return pl.pallas_call(
        place_grads_body,
        grid_spec=pltpu.PrefetchScalarGridSpec(
            num_scalar_prefetch=2,
            grid=(2, steps),
            in_specs=[pl.BlockSpec((NC // steps, 3 * BLK, BLK), lambda i, j, h, c: (j, 0, 0))],
            out_specs=[out] * 3,
        ),
        out_shape=[shape] * 3,
        compiler_params=params(),
        cost_estimate=cost(0, 9 * BLK * feats * 2),
        name="place_grads",
    )(here, chosen, back)


def along_y(x, s):
    return lax.ppermute(x, "ctx", [(c, c ^ (s * Z)) for c in range(NC)])


def along_z(x, t):
    return lax.ppermute(x, "ctx", [(c, c ^ t) for c in range(NC)])


def along_x(x, u):
    return lax.ppermute(x, "dp", [(d, d ^ (u * 4)) for d in range(16)])


def along_z_lo(x):
    return lax.ppermute(x, "dp", [(d, d ^ 2) for d in range(16)])


def along_core(x):
    return lax.ppermute(x, "dp", [(d, d ^ 1) for d in range(16)])


def spread(x, along):
    return [x] + [along(x, i) for i in (1, 2, 3)]


def swap(parts, along):
    return [parts[0]] + [along(parts[i], i) for i in (1, 2, 3)]


def shards(queries, keys, values, out_grad, chosen, proj):
    picked = chosen[0]
    ctx = lax.axis_index("ctx")
    dp = lax.axis_index("dp")
    here = jnp.stack([ctx, dp, ctx // Z, ctx % Z, dp // 4, dp % 4]).astype(jnp.int32)

    gs = take_grad(here, picked, out_grad)
    gs_y = spread(gs, along_y)
    qkv_own = take_heads(here, picked, queries, keys, values)

    rows_low = jnp.stack([proj, along_z_lo(proj)])
    rows_z, gs_y[1], gs_y[3], qkv_own = lax.optimization_barrier(
        (spread(rows_low, along_z), gs_y[1], gs_y[3], qkv_own)
    )
    rows_z = jnp.concatenate(rows_z, 0)
    rows_x = spread(rows_z, along_x)
    proj_rows = rows_x + [along_core(rows) for rows in rows_x]

    qkv = lax.all_to_all(qkv_own, "ctx", 0, 0, tiled=True)

    *grad_parts, wide = attn_grad_product(here, gs_y, proj_rows)
    qkv, grad_parts = lax.optimization_barrier((qkv, grad_parts))
    grads = swap(grad_parts, along_z)

    attn, *attn_parts, lse = attn_forward(here, picked, qkv)
    attns = swap(attn_parts, along_z)

    back = attn_backward(here, picked, qkv, grads, attn, lse)
    back, attns = lax.optimization_barrier((back, attns))
    back = lax.all_to_all(back, "ctx", 0, 0, tiled=True)

    products = proj_products(here, attns, wide, gs_y)
    mixed = swap(products[:Y], along_y)
    dw_own, dw_other = products[Y:]
    dw = swap(fold([dw_own, along_core(dw_other)], BF16), along_x)
    dw_own, dw_other = fold(dw, BF16)
    dw = swap(fold([dw_own, along_z_lo(dw_other)], F32), along_z)

    attn_out = place_mixed(here, picked, mixed)
    placed = place_grads(here, picked, back)
    dw, (q_grad, k_grad, v_grad) = lax.optimization_barrier((dw, placed))
    proj_grad = dw[0] + dw[1] + dw[2] + dw[3]
    return attn_out, q_grad, k_grad, v_grad, proj_grad


def solution(mesh):
    rows = P("dp", "ctx", None)
    return jax.shard_map(
        shards,
        mesh=mesh,
        in_specs=(rows, rows, rows, rows, P("dp", None), P("ctx", "dp")),
        out_specs=(rows, rows, rows, rows, P("ctx", "dp")),
        check_vma=False,
    )
```

```python
import functools
import math

import jax
import jax.numpy as jnp
from jax import lax
from jax.experimental import pallas as pl
from jax.experimental.pallas import tpu as pltpu
from jax.sharding import PartitionSpec as P

BLK = 128
Y = 4
Z = 4
NC = Y * Z
PAIR = 2 * BLK
NEG = -1e30
VMEM_BYTES = 48 * 1024 * 1024
F32 = jnp.float32
BF16 = jnp.bfloat16


def dot_nt(a, b):
    return lax.dot_general(a, b, (((1,), (1,)), ((), ())), preferred_element_type=F32)


def dot_nn(a, b):
    return lax.dot_general(a, b, (((1,), (0,)), ((), ())), preferred_element_type=F32)


def params():
    return pltpu.CompilerParams(vmem_limit_bytes=VMEM_BYTES)


def cost(flops, nbytes, trans=0):
    return pl.CostEstimate(flops=flops, bytes_accessed=nbytes, transcendentals=trans)


def half_of(here_ref, chosen_ref):
    pick = chosen_ref[here_ref[0]]
    return ((pick >= 0) & (pick != here_ref[0])).astype(jnp.int32)


def take_body(here_ref, chosen_ref, q_ref, k_ref, v_ref, qkv_ref):
    live = chosen_ref[here_ref[0]] >= 0
    zero = jnp.zeros((), BF16)
    heads = qkv_ref.shape[0]
    for h in range(heads):
        cols = slice(h * BLK, (h + 1) * BLK)
        for part, src in enumerate((q_ref, k_ref, v_ref)):
            qkv_ref[h, part * BLK : (part + 1) * BLK, :] = jnp.where(live, src[0, :, cols], zero)


def take_heads(here, chosen, queries, keys, values):
    feats = queries.shape[2]
    steps = 2
    width = feats // steps
    src = pl.BlockSpec((1, BLK, width), lambda i, h, c: (0, half_of(h, c), i))
    return pl.pallas_call(
        take_body,
        grid_spec=pltpu.PrefetchScalarGridSpec(
            num_scalar_prefetch=2,
            grid=(steps,),
            in_specs=[src] * 3,
            out_specs=pl.BlockSpec((NC // steps, 3 * BLK, BLK), lambda i, h, c: (i, 0, 0)),
        ),
        out_shape=jax.ShapeDtypeStruct((NC, 3 * BLK, BLK), BF16),
        compiler_params=pltpu.CompilerParams(vmem_limit_bytes=62 * 1024 * 1024),
        cost_estimate=cost(0, 6 * BLK * feats * 2),
        name="take_heads",
    )(here, chosen, queries, keys, values)


def take_grad_body(here_ref, chosen_ref, g_ref, gs_ref):
    live = chosen_ref[here_ref[0]] >= 0
    gs_ref[...] = jnp.where(live, g_ref[0], jnp.zeros((), BF16))


def take_grad(here, chosen, out_grad):
    feats = out_grad.shape[2]
    return pl.pallas_call(
        take_grad_body,
        grid_spec=pltpu.PrefetchScalarGridSpec(
            num_scalar_prefetch=2,
            grid=(2,),
            in_specs=[pl.BlockSpec((1, BLK // 2, feats), lambda i, h, c: (0, 2 * half_of(h, c) + i, 0))],
            out_specs=pl.BlockSpec((BLK // 2, feats), lambda i, h, c: (i, 0)),
        ),
        out_shape=jax.ShapeDtypeStruct((BLK, feats), BF16),
        compiler_params=pltpu.CompilerParams(vmem_limit_bytes=62 * 1024 * 1024),
        cost_estimate=cost(0, 2 * BLK * feats * 2),
        name="take_grad",
    )(here, chosen, out_grad)


def attn_grad_body(here_ref, *refs):
    g_refs, w_refs, outs, wide_ref = refs[:Y], refs[Y : Y + 8], refs[Y + 8 : Y + 8 + Z], refs[-1]
    x, k = here_ref[4], here_ref[5]
    for u in range(4):
        for v in range(4):
            d = (x ^ u) * 4 + (k ^ v)
            cols = pl.ds(pl.multiple_of(d * BLK, BLK), BLK)
            for t in range(Z):
                wide_ref[t * BLK : (t + 1) * BLK, cols] = w_refs[4 * (v % 2) + u][t * 2 + v // 2]
    for t in range(Z):
        for s in range(Y):
            outs[t][s] = dot_nt(g_refs[s][...], wide_ref[t * BLK : (t + 1) * BLK, :]).astype(BF16)


def attn_grad_product(here, grads, proj_rows):
    cols = grads[0].shape[1]
    vmem = pl.BlockSpec(memory_space=pltpu.VMEM)
    return pl.pallas_call(
        attn_grad_body,
        in_specs=[pl.BlockSpec(memory_space=pltpu.SMEM)] + [vmem] * (Y + 8),
        out_shape=[jax.ShapeDtypeStruct((Y, BLK, BLK), BF16)] * Z
        + [jax.ShapeDtypeStruct((Z * BLK, cols), BF16)],
        compiler_params=params(),
        cost_estimate=cost(2 * 512 * 512 * cols, 3 * 512 * cols * 2),
        name="attn_grad_product",
    )(here, *grads, *proj_rows)


def sort_blocks(chosen_ref, order_ref):
    count = jnp.int32(0)
    for pos in range(2 * NC):
        c = pos if pos < NC else 2 * NC - 1 - pos
        hit = chosen_ref[c] == pos

        @pl.when(hit)
        def _():
            order_ref[count] = c

        count = count + hit.astype(jnp.int32)
    live = count
    for c in range(NC):
        hit = chosen_ref[c] < 0

        @pl.when(hit)
        def _():
            order_ref[count] = c

        count = count + hit.astype(jnp.int32)
    return live


def causal(s):
    key = lax.broadcasted_iota(jnp.int32, s.shape, 0)
    query = lax.broadcasted_iota(jnp.int32, s.shape, 1)
    return jnp.where(key <= query, s, NEG)


def forward_body(
    here_ref, chosen_ref, qkv_ref, attn_ref, out0, out1, out2, out3, lse_ref, q_s, k_s, vt_s, order_ref
):
    a, b = here_ref[2], here_ref[3]
    live = sort_blocks(chosen_ref, order_ref)
    scale2 = math.log2(math.e) / math.sqrt(BLK)
    for r in range(NC):
        c = order_ref[r]
        rows = slice(r * BLK, (r + 1) * BLK)

        @pl.when(r // 2 * 2 < live)
        def _():
            q_s[rows, :] = qkv_ref[c, 0:BLK, :]
            k_s[rows, :] = qkv_ref[c, BLK : 2 * BLK, :]
            vt_s[:, rows] = qkv_ref[c, 2 * BLK : 3 * BLK, :].T

        @pl.when(r >= live)
        def _():
            attn_ref[b ^ (c % Z), a ^ (c // Z)] = jnp.zeros((BLK, BLK), BF16)

    for p in range(NC // 2):

        @pl.when(2 * p < live)
        def _():
            low = p * PAIR
            q2 = q_s[low : low + PAIR, :]
            diag = causal(dot_nt(k_s[low : low + PAIR, :], q2))
            parts = [(low, diag)]
            top = jnp.max(diag, axis=0, keepdims=True)
            for j in range(p):
                s = dot_nt(k_s[j * PAIR : (j + 1) * PAIR, :], q2)
                top = jnp.maximum(top, jnp.max(s, axis=0, keepdims=True))
                parts.append((j * PAIR, s))
            total = jnp.zeros((1, PAIR), F32)
            out_t = jnp.zeros((BLK, PAIR), F32)
            shift = top * scale2
            for start, s in parts:
                e = jnp.exp2(s * scale2 - shift)
                total = total + jnp.sum(e, axis=0, keepdims=True)
                out_t = out_t + dot_nn(vt_s[:, start : start + PAIR], e.astype(BF16))
            lse_ref[p : p + 1, :] = shift + jnp.log2(total)
            out = (out_t * (1.0 / total)).T.astype(BF16)
            for t in range(2):
                c = order_ref[2 * p + t]

                @pl.when(2 * p + t < live)
                def _():
                    attn_ref[b ^ (c % Z), a ^ (c // Z)] = out[t * BLK : (t + 1) * BLK, :]

    for t, out_ref in enumerate((out0, out1, out2, out3)):
        out_ref[...] = attn_ref[t]


def attn_forward(here, chosen, qkv):
    slots = NC * BLK
    return pl.pallas_call(
        forward_body,
        in_specs=[
            pl.BlockSpec(memory_space=pltpu.SMEM),
            pl.BlockSpec(memory_space=pltpu.SMEM),
            pl.BlockSpec(memory_space=pltpu.VMEM),
        ],
        out_shape=[jax.ShapeDtypeStruct((Z, Y, BLK, BLK), BF16)]
        + [jax.ShapeDtypeStruct((Y, BLK, BLK), BF16)] * Z
        + [
            jax.ShapeDtypeStruct((NC // 2, PAIR), F32),
        ],
        scratch_shapes=[
            pltpu.VMEM((slots, BLK), BF16),
            pltpu.VMEM((slots, BLK), BF16),
            pltpu.VMEM((BLK, slots), BF16),
            pltpu.SMEM((NC,), jnp.int32),
        ],
        compiler_params=params(),
        cost_estimate=cost(2 * 2 * slots * slots * BLK, 4 * slots * BLK * 2, slots * slots),
        name="attn_forward",
    )(here, chosen, qkv)


def backward_body(
    here_ref,
    chosen_ref,
    qkv_ref,
    grad0,
    grad1,
    grad2,
    grad3,
    attn_ref,
    lse_ref,
    out_ref,
    q_s,
    k_s,
    v_s,
    g_s,
    kt_s,
    dk_s,
    dv_s,
    grad_ref,
    order_ref,
):
    a, b = here_ref[2], here_ref[3]
    for t, part in enumerate((grad0, grad1, grad2, grad3)):
        grad_ref[t] = part[...]
    live = sort_blocks(chosen_ref, order_ref)
    scale = 1.0 / math.sqrt(BLK)
    scale2 = math.log2(math.e) * scale
    for r in range(NC):
        c = order_ref[r]
        rows = slice(r * BLK, (r + 1) * BLK)

        @pl.when(r // 2 * 2 < live)
        def _():
            k_blk = qkv_ref[c, BLK : 2 * BLK, :]
            q_s[rows, :] = qkv_ref[c, 0:BLK, :]
            k_s[rows, :] = k_blk
            kt_s[:, rows] = k_blk.T
            v_s[rows, :] = qkv_ref[c, 2 * BLK : 3 * BLK, :]
            g_s[rows, :] = grad_ref[b ^ (c % Z), a ^ (c // Z)]

        @pl.when(r >= live)
        def _():
            out_ref[c] = jnp.zeros((3 * BLK, BLK), BF16)

    for p in range(NC // 2):

        @pl.when(2 * p < live)
        def _():
            low = p * PAIR
            q2 = q_s[low : low + PAIR, :]
            g2 = g_s[low : low + PAIR, :]
            deltas = []
            for t in range(2):
                c = order_ref[2 * p + t]
                prod = g2[t * BLK : (t + 1) * BLK, :].astype(F32) * attn_ref[b ^ (c % Z), a ^ (c // Z)].astype(F32)
                deltas.append(jnp.sum(prod.T, axis=0, keepdims=True))
            delta = jnp.concatenate(deltas, axis=1)
            lse = lse_ref[p : p + 1, :]
            dq_t = jnp.zeros((BLK, PAIR), F32)
            for j in range(p + 1):
                keys = slice(j * PAIR, (j + 1) * PAIR)
                s = dot_nt(k_s[keys, :], q2)
                if j == p:
                    s = causal(s)
                prob = jnp.exp2(s * scale2 - lse)
                dprob = dot_nt(v_s[keys, :], g2)
                ds = (prob * (dprob - delta)).astype(BF16)
                dv = dot_nn(prob.astype(BF16), g2)
                dk = dot_nn(ds, q2)
                if j == p:
                    dv_s[keys, :] = dv
                    dk_s[keys, :] = dk
                else:
                    dv_s[keys, :] += dv
                    dk_s[keys, :] += dk
                dq_t = dq_t + dot_nn(kt_s[:, keys], ds)
            dq = (dq_t * scale).T.astype(BF16)
            for t in range(2):
                c = order_ref[2 * p + t]

                @pl.when(2 * p + t < live)
                def _():
                    out_ref[c, 0:BLK, :] = dq[t * BLK : (t + 1) * BLK, :]

    for r in range(NC):
        c = order_ref[r]
        rows = slice(r * BLK, (r + 1) * BLK)

        @pl.when(r < live)
        def _():
            out_ref[c, BLK : 2 * BLK, :] = (dk_s[rows, :] * scale).astype(BF16)
            out_ref[c, 2 * BLK : 3 * BLK, :] = dv_s[rows, :].astype(BF16)


def attn_backward(here, chosen, qkv, grads, attn, lse):
    slots = NC * BLK
    return pl.pallas_call(
        backward_body,
        in_specs=[pl.BlockSpec(memory_space=pltpu.SMEM)] * 2 + [pl.BlockSpec(memory_space=pltpu.VMEM)] * 7,
        out_shape=jax.ShapeDtypeStruct((NC, 3 * BLK, BLK), BF16),
        scratch_shapes=[
            pltpu.VMEM((slots, BLK), BF16),
            pltpu.VMEM((slots, BLK), BF16),
            pltpu.VMEM((slots, BLK), BF16),
            pltpu.VMEM((slots, BLK), BF16),
            pltpu.VMEM((BLK, slots), BF16),
            pltpu.VMEM((slots, BLK), F32),
            pltpu.VMEM((slots, BLK), F32),
            pltpu.VMEM((Z, Y, BLK, BLK), BF16),
            pltpu.SMEM((NC,), jnp.int32),
        ],
        compiler_params=params(),
        cost_estimate=cost(5 * 2 * slots * slots * BLK, 8 * slots * BLK * 2, slots * slots),
        name="attn_backward",
    )(here, chosen, qkv, *grads, attn, lse)


def dw_body(here_ref, *refs):
    attn_refs, g_refs, dw_refs = refs[:Z], refs[Z : Z + Y], refs[Z + Y : Z + Y + 2]
    at_s, g_s, dw_s = refs[-3:]
    x, k = here_ref[4], here_ref[5]
    for t in range(Z):
        for s in range(Y):
            at_s[t * BLK : (t + 1) * BLK, s * BLK : (s + 1) * BLK] = attn_refs[t][s].T
    for s in range(Y):
        g_s[s * BLK : (s + 1) * BLK, :] = g_refs[s][...]
    width = g_s.shape[1] // 4
    for u in range(4):
        cols = pl.ds(pl.multiple_of((x ^ u) * width, width), width)
        for t in range(Z):
            part = dot_nn(at_s[t * BLK : (t + 1) * BLK, :], g_s[:, cols]).astype(BF16)
            for j in range(4):
                dw_s[u, j, t] = part[:, j * BLK : (j + 1) * BLK]
    for core, dw_ref in enumerate(dw_refs):
        for low in range(2):
            dw_ref[:, low] = dw_s[:, k ^ (2 * low + core)]


def dw_product(here, attns, grads):
    cols = grads[0].shape[1]
    vmem = pl.BlockSpec(memory_space=pltpu.VMEM)
    return pl.pallas_call(
        dw_body,
        in_specs=[pl.BlockSpec(memory_space=pltpu.SMEM)] + [vmem] * 8,
        out_shape=[jax.ShapeDtypeStruct((4, 2, Z, BLK, BLK), BF16)] * 2,
        scratch_shapes=[
            pltpu.VMEM((Z * BLK, Y * BLK), BF16),
            pltpu.VMEM((Y * BLK, cols), BF16),
            pltpu.VMEM((4, 4, Z, BLK, BLK), BF16),
        ],
        compiler_params=params(),
        cost_estimate=cost(2 * 512 * 512 * cols, 2 * 512 * cols * 2),
        name="dw_product",
    )(here, *attns, *grads)


def mix_body(*refs):
    attn_refs, wide_ref, mix_refs, a_s = refs[:Z], refs[Z], refs[Z + 1 : Z + 1 + Y], refs[-1]
    for t in range(Z):
        for s in range(Y):
            a_s[s * BLK : (s + 1) * BLK, t * BLK : (t + 1) * BLK] = attn_refs[t][s]
    width = wide_ref.shape[1] // 4
    for j in range(4):
        cols = slice(j * width, (j + 1) * width)
        for s in range(Y):
            mix_refs[s][:, cols] = dot_nn(a_s[s * BLK : (s + 1) * BLK, :], wide_ref[:, cols]).astype(BF16)


def mix_product(attns, wide):
    cols = wide.shape[1]
    return pl.pallas_call(
        mix_body,
        out_shape=[jax.ShapeDtypeStruct((BLK, cols), BF16)] * Y,
        scratch_shapes=[pltpu.VMEM((Y * BLK, Z * BLK), BF16)],
        compiler_params=params(),
        cost_estimate=cost(2 * 512 * 512 * cols, 2 * 512 * cols * 2),
        name="mix_product",
    )(*attns, wide)


def fold_body(count, *refs):
    ins, outs = refs[:count], refs[count:]
    for i, out in enumerate(outs):
        total = ins[0][i].astype(F32)
        for part in ins[1:]:
            total = total + part[i].astype(F32)
        out[...] = total.astype(out.dtype)


def fold(parts, kind):
    shape = parts[0].shape
    return pl.pallas_call(
        functools.partial(fold_body, len(parts)),
        out_shape=[jax.ShapeDtypeStruct(shape[1:], kind)] * shape[0],
        compiler_params=params(),
        cost_estimate=cost(0, 5 * math.prod(shape) * 2),
        name="fold",
    )(*parts)


def place_mixed_body(here_ref, chosen_ref, p0, p1, p2, p3, out_ref):
    mine = pl.program_id(0) == half_of(here_ref, chosen_ref)

    @pl.when(mine)
    def _():
        total = p0[...].astype(F32) + p1[...].astype(F32) + p2[...].astype(F32) + p3[...].astype(F32)
        out_ref[0] = total.astype(BF16)

    @pl.when(jnp.logical_not(mine))
    def _():
        out_ref[...] = jnp.zeros(out_ref.shape, BF16)


def place_mixed(here, chosen, parts):
    cols = parts[0].shape[1]
    steps = 2
    width = cols // steps
    return pl.pallas_call(
        place_mixed_body,
        grid_spec=pltpu.PrefetchScalarGridSpec(
            num_scalar_prefetch=2,
            grid=(2, steps),
            in_specs=[pl.BlockSpec((BLK, width), lambda i, j, h, c: (0, j))] * Y,
            out_specs=pl.BlockSpec((1, BLK, width), lambda i, j, h, c: (0, i, j)),
        ),
        out_shape=jax.ShapeDtypeStruct((1, 2 * BLK, cols), BF16),
        compiler_params=params(),
        cost_estimate=cost(0, 6 * BLK * cols * 2),
        name="place_mixed",
    )(here, chosen, *parts)


def place_grads_body(here_ref, chosen_ref, back_ref, q_ref, k_ref, v_ref):
    mine = pl.program_id(0) == half_of(here_ref, chosen_ref)
    heads = back_ref.shape[0]

    @pl.when(mine)
    def _():
        for h in range(heads):
            cols = slice(h * BLK, (h + 1) * BLK)
            for part, out in enumerate((q_ref, k_ref, v_ref)):
                out[0, :, cols] = back_ref[h, part * BLK : (part + 1) * BLK, :]

    @pl.when(jnp.logical_not(mine))
    def _():
        for out in (q_ref, k_ref, v_ref):
            out[...] = jnp.zeros(out.shape, BF16)


def place_grads(here, chosen, back):
    feats = NC * BLK
    steps = 2
    width = feats // steps
    out = pl.BlockSpec((1, BLK, width), lambda i, j, h, c: (0, i, j))
    shape = jax.ShapeDtypeStruct((1, 2 * BLK, feats), BF16)
    return pl.pallas_call(
        place_grads_body,
        grid_spec=pltpu.PrefetchScalarGridSpec(
            num_scalar_prefetch=2,
            grid=(2, steps),
            in_specs=[pl.BlockSpec((NC // steps, 3 * BLK, BLK), lambda i, j, h, c: (j, 0, 0))],
            out_specs=[out] * 3,
        ),
        out_shape=[shape] * 3,
        compiler_params=params(),
        cost_estimate=cost(0, 9 * BLK * feats * 2),
        name="place_grads",
    )(here, chosen, back)


def along_y(x, s):
    return lax.ppermute(x, "ctx", [(c, c ^ (s * Z)) for c in range(NC)])


def along_z(x, t):
    return lax.ppermute(x, "ctx", [(c, c ^ t) for c in range(NC)])


def along_x(x, u):
    return lax.ppermute(x, "dp", [(d, d ^ (u * 4)) for d in range(16)])


def along_z_lo(x):
    return lax.ppermute(x, "dp", [(d, d ^ 2) for d in range(16)])


def along_core(x):
    return lax.ppermute(x, "dp", [(d, d ^ 1) for d in range(16)])


def spread(x, along):
    return [x] + [along(x, i) for i in (1, 2, 3)]


def swap(parts, along):
    return [parts[0]] + [along(parts[i], i) for i in (1, 2, 3)]


def shards(queries, keys, values, out_grad, chosen, proj):
    picked = chosen[0]
    ctx = lax.axis_index("ctx")
    dp = lax.axis_index("dp")
    here = jnp.stack([ctx, dp, ctx // Z, ctx % Z, dp // 4, dp % 4]).astype(jnp.int32)

    gs = take_grad(here, picked, out_grad)
    gs_y = spread(gs, along_y)
    qkv_own = take_heads(here, picked, queries, keys, values)

    rows_low = jnp.stack([proj, along_z_lo(proj)])
    rows_z, gs_y[1], gs_y[3], qkv_own = lax.optimization_barrier(
        (spread(rows_low, along_z), gs_y[1], gs_y[3], qkv_own)
    )
    rows_z = jnp.concatenate(rows_z, 0)
    rows_x = spread(rows_z, along_x)
    proj_rows = rows_x + [along_core(rows) for rows in rows_x]

    qkv = lax.all_to_all(qkv_own, "ctx", 0, 0, tiled=True)

    *grad_parts, wide = attn_grad_product(here, gs_y, proj_rows)
    grads = swap(grad_parts, along_z)
    qkv, grads[0] = lax.optimization_barrier((qkv, grads[0]))

    attn, *attn_parts, lse = attn_forward(here, picked, qkv)
    attns = swap(attn_parts, along_z)

    back = attn_backward(here, picked, qkv, grads, attn, lse)
    back, attns = lax.optimization_barrier((back, attns))
    back = lax.all_to_all(back, "ctx", 0, 0, tiled=True)

    dw_own, dw_other = dw_product(here, attns, gs_y)
    wide, dw_other = lax.optimization_barrier((wide, dw_other))
    mixed = swap(mix_product(attns, wide), along_y)
    dw = swap(fold([dw_own, along_core(dw_other)], BF16), along_x)
    dw_own, dw_other = fold(dw, BF16)
    dw = swap(fold([dw_own, along_z_lo(dw_other)], F32), along_z)

    attn_out = place_mixed(here, picked, mixed)
    placed = place_grads(here, picked, back)
    dw, (q_grad, k_grad, v_grad) = lax.optimization_barrier((dw, placed))
    proj_grad = dw[0] + dw[1] + dw[2] + dw[3]
    return attn_out, q_grad, k_grad, v_grad, proj_grad


def solution(mesh):
    rows = P("dp", "ctx", None)
    return jax.shard_map(
        shards,
        mesh=mesh,
        in_specs=(rows, rows, rows, rows, P("dp", None), P("ctx", "dp")),
        out_specs=(rows, rows, rows, rows, P("ctx", "dp")),
        check_vma=False,
    )
```

```python
import functools
import math

import jax
import jax.numpy as jnp
from jax import lax
from jax.experimental import pallas as pl
from jax.experimental.pallas import tpu as pltpu
from jax.sharding import PartitionSpec as P

BLK = 128
Y = 4
Z = 4
NC = Y * Z
PAIR = 2 * BLK
NEG = -1e30
VMEM_BYTES = 48 * 1024 * 1024
F32 = jnp.float32
BF16 = jnp.bfloat16


def dot_nt(a, b):
    return lax.dot_general(a, b, (((1,), (1,)), ((), ())), preferred_element_type=F32)


def dot_nn(a, b):
    return lax.dot_general(a, b, (((1,), (0,)), ((), ())), preferred_element_type=F32)


def params():
    return pltpu.CompilerParams(vmem_limit_bytes=VMEM_BYTES)


def cost(flops, nbytes, trans=0):
    return pl.CostEstimate(flops=flops, bytes_accessed=nbytes, transcendentals=trans)


def half_of(here_ref, chosen_ref):
    pick = chosen_ref[here_ref[0]]
    return ((pick >= 0) & (pick != here_ref[0])).astype(jnp.int32)


def take_body(here_ref, chosen_ref, q_ref, k_ref, v_ref, qkv_ref):
    live = chosen_ref[here_ref[0]] >= 0
    zero = jnp.zeros((), BF16)
    heads = qkv_ref.shape[0]
    for h in range(heads):
        cols = slice(h * BLK, (h + 1) * BLK)
        for part, src in enumerate((q_ref, k_ref, v_ref)):
            qkv_ref[h, part * BLK : (part + 1) * BLK, :] = jnp.where(live, src[0, :, cols], zero)


def take_heads(here, chosen, queries, keys, values):
    feats = queries.shape[2]
    steps = 1
    width = feats // steps
    src = pl.BlockSpec((1, BLK, width), lambda i, h, c: (0, half_of(h, c), i))
    return pl.pallas_call(
        take_body,
        grid_spec=pltpu.PrefetchScalarGridSpec(
            num_scalar_prefetch=2,
            grid=(steps,),
            in_specs=[src] * 3,
            out_specs=pl.BlockSpec((NC // steps, 3 * BLK, BLK), lambda i, h, c: (i, 0, 0)),
        ),
        out_shape=jax.ShapeDtypeStruct((NC, 3 * BLK, BLK), BF16),
        compiler_params=pltpu.CompilerParams(vmem_limit_bytes=62 * 1024 * 1024),
        cost_estimate=cost(0, 6 * BLK * feats * 2),
        name="take_heads",
    )(here, chosen, queries, keys, values)


def take_grad_body(here_ref, chosen_ref, g_ref, gs_ref):
    live = chosen_ref[here_ref[0]] >= 0
    gs_ref[...] = jnp.where(live, g_ref[0], jnp.zeros((), BF16))


def take_grad(here, chosen, out_grad):
    feats = out_grad.shape[2]
    return pl.pallas_call(
        take_grad_body,
        grid_spec=pltpu.PrefetchScalarGridSpec(
            num_scalar_prefetch=2,
            grid=(2,),
            in_specs=[pl.BlockSpec((1, BLK // 2, feats), lambda i, h, c: (0, 2 * half_of(h, c) + i, 0))],
            out_specs=pl.BlockSpec((BLK // 2, feats), lambda i, h, c: (i, 0)),
        ),
        out_shape=jax.ShapeDtypeStruct((BLK, feats), BF16),
        compiler_params=pltpu.CompilerParams(vmem_limit_bytes=62 * 1024 * 1024),
        cost_estimate=cost(0, 2 * BLK * feats * 2),
        name="take_grad",
    )(here, chosen, out_grad)


def attn_grad_body(here_ref, *refs):
    g_refs, w_refs, outs, wide_ref = refs[:Y], refs[Y : Y + 8], refs[Y + 8 : Y + 8 + Z], refs[-1]
    x, k = here_ref[4], here_ref[5]
    for u in range(4):
        for v in range(4):
            d = (x ^ u) * 4 + (k ^ v)
            cols = pl.ds(pl.multiple_of(d * BLK, BLK), BLK)
            for t in range(Z):
                wide_ref[t * BLK : (t + 1) * BLK, cols] = w_refs[4 * (v % 2) + u][t * 2 + v // 2]
    for t in range(Z):
        for s in range(Y):
            outs[t][s] = dot_nt(g_refs[s][...], wide_ref[t * BLK : (t + 1) * BLK, :]).astype(BF16)


def attn_grad_product(here, grads, proj_rows):
    cols = grads[0].shape[1]
    vmem = pl.BlockSpec(memory_space=pltpu.VMEM)
    return pl.pallas_call(
        attn_grad_body,
        in_specs=[pl.BlockSpec(memory_space=pltpu.SMEM)] + [vmem] * (Y + 8),
        out_shape=[jax.ShapeDtypeStruct((Y, BLK, BLK), BF16)] * Z
        + [jax.ShapeDtypeStruct((Z * BLK, cols), BF16)],
        compiler_params=params(),
        cost_estimate=cost(2 * 512 * 512 * cols, 3 * 512 * cols * 2),
        name="attn_grad_product",
    )(here, *grads, *proj_rows)


def sort_blocks(chosen_ref, order_ref):
    count = jnp.int32(0)
    for pos in range(2 * NC):
        c = pos if pos < NC else 2 * NC - 1 - pos
        hit = chosen_ref[c] == pos

        @pl.when(hit)
        def _():
            order_ref[count] = c

        count = count + hit.astype(jnp.int32)
    live = count
    for c in range(NC):
        hit = chosen_ref[c] < 0

        @pl.when(hit)
        def _():
            order_ref[count] = c

        count = count + hit.astype(jnp.int32)
    return live


def causal(s):
    key = lax.broadcasted_iota(jnp.int32, s.shape, 0)
    query = lax.broadcasted_iota(jnp.int32, s.shape, 1)
    return jnp.where(key <= query, s, NEG)


def forward_body(
    here_ref, chosen_ref, qkv_ref, attn_ref, out0, out1, out2, out3, lse_ref, q_s, k_s, vt_s, order_ref
):
    a, b = here_ref[2], here_ref[3]
    live = sort_blocks(chosen_ref, order_ref)
    scale2 = math.log2(math.e) / math.sqrt(BLK)
    for r in range(NC):
        c = order_ref[r]
        rows = slice(r * BLK, (r + 1) * BLK)

        @pl.when(r // 2 * 2 < live)
        def _():
            q_s[rows, :] = qkv_ref[c, 0:BLK, :]
            k_s[rows, :] = qkv_ref[c, BLK : 2 * BLK, :]
            vt_s[:, rows] = qkv_ref[c, 2 * BLK : 3 * BLK, :].T

        @pl.when(r >= live)
        def _():
            attn_ref[b ^ (c % Z), a ^ (c // Z)] = jnp.zeros((BLK, BLK), BF16)

    for p in range(NC // 2):

        @pl.when(2 * p < live)
        def _():
            low = p * PAIR
            q2 = q_s[low : low + PAIR, :]
            diag = causal(dot_nt(k_s[low : low + PAIR, :], q2))
            parts = [(low, diag)]
            top = jnp.max(diag, axis=0, keepdims=True)
            for j in range(p):
                s = dot_nt(k_s[j * PAIR : (j + 1) * PAIR, :], q2)
                top = jnp.maximum(top, jnp.max(s, axis=0, keepdims=True))
                parts.append((j * PAIR, s))
            total = jnp.zeros((1, PAIR), F32)
            out_t = jnp.zeros((BLK, PAIR), F32)
            shift = top * scale2
            for start, s in parts:
                e = jnp.exp2(s * scale2 - shift)
                total = total + jnp.sum(e, axis=0, keepdims=True)
                out_t = out_t + dot_nn(vt_s[:, start : start + PAIR], e.astype(BF16))
            lse_ref[p : p + 1, :] = shift + jnp.log2(total)
            out = (out_t * (1.0 / total)).T.astype(BF16)
            for t in range(2):
                c = order_ref[2 * p + t]

                @pl.when(2 * p + t < live)
                def _():
                    attn_ref[b ^ (c % Z), a ^ (c // Z)] = out[t * BLK : (t + 1) * BLK, :]

    for t, out_ref in enumerate((out0, out1, out2, out3)):
        out_ref[...] = attn_ref[t]


def attn_forward(here, chosen, qkv):
    slots = NC * BLK
    return pl.pallas_call(
        forward_body,
        in_specs=[
            pl.BlockSpec(memory_space=pltpu.SMEM),
            pl.BlockSpec(memory_space=pltpu.SMEM),
            pl.BlockSpec(memory_space=pltpu.VMEM),
        ],
        out_shape=[jax.ShapeDtypeStruct((Z, Y, BLK, BLK), BF16)]
        + [jax.ShapeDtypeStruct((Y, BLK, BLK), BF16)] * Z
        + [
            jax.ShapeDtypeStruct((NC // 2, PAIR), F32),
        ],
        scratch_shapes=[
            pltpu.VMEM((slots, BLK), BF16),
            pltpu.VMEM((slots, BLK), BF16),
            pltpu.VMEM((BLK, slots), BF16),
            pltpu.SMEM((NC,), jnp.int32),
        ],
        compiler_params=params(),
        cost_estimate=cost(2 * 2 * slots * slots * BLK, 4 * slots * BLK * 2, slots * slots),
        name="attn_forward",
    )(here, chosen, qkv)


def backward_body(
    here_ref,
    chosen_ref,
    qkv_ref,
    grad0,
    grad1,
    grad2,
    grad3,
    attn_ref,
    lse_ref,
    out_ref,
    q_s,
    k_s,
    v_s,
    g_s,
    kt_s,
    dk_s,
    dv_s,
    grad_ref,
    order_ref,
):
    a, b = here_ref[2], here_ref[3]
    for t, part in enumerate((grad0, grad1, grad2, grad3)):
        grad_ref[t] = part[...]
    live = sort_blocks(chosen_ref, order_ref)
    scale = 1.0 / math.sqrt(BLK)
    scale2 = math.log2(math.e) * scale
    for r in range(NC):
        c = order_ref[r]
        rows = slice(r * BLK, (r + 1) * BLK)

        @pl.when(r // 2 * 2 < live)
        def _():
            k_blk = qkv_ref[c, BLK : 2 * BLK, :]
            q_s[rows, :] = qkv_ref[c, 0:BLK, :]
            k_s[rows, :] = k_blk
            kt_s[:, rows] = k_blk.T
            v_s[rows, :] = qkv_ref[c, 2 * BLK : 3 * BLK, :]
            g_s[rows, :] = grad_ref[b ^ (c % Z), a ^ (c // Z)]

        @pl.when(r >= live)
        def _():
            out_ref[c] = jnp.zeros((3 * BLK, BLK), BF16)

    for p in range(NC // 2):

        @pl.when(2 * p < live)
        def _():
            low = p * PAIR
            q2 = q_s[low : low + PAIR, :]
            g2 = g_s[low : low + PAIR, :]
            deltas = []
            for t in range(2):
                c = order_ref[2 * p + t]
                prod = g2[t * BLK : (t + 1) * BLK, :].astype(F32) * attn_ref[b ^ (c % Z), a ^ (c // Z)].astype(F32)
                deltas.append(jnp.sum(prod.T, axis=0, keepdims=True))
            delta = jnp.concatenate(deltas, axis=1)
            lse = lse_ref[p : p + 1, :]
            dq_t = jnp.zeros((BLK, PAIR), F32)
            for j in range(p + 1):
                keys = slice(j * PAIR, (j + 1) * PAIR)
                s = dot_nt(k_s[keys, :], q2)
                if j == p:
                    s = causal(s)
                prob = jnp.exp2(s * scale2 - lse)
                dprob = dot_nt(v_s[keys, :], g2)
                ds = (prob * (dprob - delta)).astype(BF16)
                dv = dot_nn(prob.astype(BF16), g2)
                dk = dot_nn(ds, q2)
                if j == p:
                    dv_s[keys, :] = dv
                    dk_s[keys, :] = dk
                else:
                    dv_s[keys, :] += dv
                    dk_s[keys, :] += dk
                dq_t = dq_t + dot_nn(kt_s[:, keys], ds)
            dq = (dq_t * scale).T.astype(BF16)
            for t in range(2):
                c = order_ref[2 * p + t]

                @pl.when(2 * p + t < live)
                def _():
                    out_ref[c, 0:BLK, :] = dq[t * BLK : (t + 1) * BLK, :]

    for r in range(NC):
        c = order_ref[r]
        rows = slice(r * BLK, (r + 1) * BLK)

        @pl.when(r < live)
        def _():
            out_ref[c, BLK : 2 * BLK, :] = (dk_s[rows, :] * scale).astype(BF16)
            out_ref[c, 2 * BLK : 3 * BLK, :] = dv_s[rows, :].astype(BF16)


def attn_backward(here, chosen, qkv, grads, attn, lse):
    slots = NC * BLK
    return pl.pallas_call(
        backward_body,
        in_specs=[pl.BlockSpec(memory_space=pltpu.SMEM)] * 2 + [pl.BlockSpec(memory_space=pltpu.VMEM)] * 7,
        out_shape=jax.ShapeDtypeStruct((NC, 3 * BLK, BLK), BF16),
        scratch_shapes=[
            pltpu.VMEM((slots, BLK), BF16),
            pltpu.VMEM((slots, BLK), BF16),
            pltpu.VMEM((slots, BLK), BF16),
            pltpu.VMEM((slots, BLK), BF16),
            pltpu.VMEM((BLK, slots), BF16),
            pltpu.VMEM((slots, BLK), F32),
            pltpu.VMEM((slots, BLK), F32),
            pltpu.VMEM((Z, Y, BLK, BLK), BF16),
            pltpu.SMEM((NC,), jnp.int32),
        ],
        compiler_params=params(),
        cost_estimate=cost(5 * 2 * slots * slots * BLK, 8 * slots * BLK * 2, slots * slots),
        name="attn_backward",
    )(here, chosen, qkv, *grads, attn, lse)


def dw_body(here_ref, *refs):
    attn_refs, g_refs, dw_refs = refs[:Z], refs[Z : Z + Y], refs[Z + Y : Z + Y + 2]
    at_s, g_s, dw_s = refs[-3:]
    x, k = here_ref[4], here_ref[5]
    for t in range(Z):
        for s in range(Y):
            at_s[t * BLK : (t + 1) * BLK, s * BLK : (s + 1) * BLK] = attn_refs[t][s].T
    for s in range(Y):
        g_s[s * BLK : (s + 1) * BLK, :] = g_refs[s][...]
    width = g_s.shape[1] // 4
    for u in range(4):
        cols = pl.ds(pl.multiple_of((x ^ u) * width, width), width)
        for t in range(Z):
            part = dot_nn(at_s[t * BLK : (t + 1) * BLK, :], g_s[:, cols]).astype(BF16)
            for j in range(4):
                dw_s[u, j, t] = part[:, j * BLK : (j + 1) * BLK]
    for core, dw_ref in enumerate(dw_refs):
        for low in range(2):
            dw_ref[:, low] = dw_s[:, k ^ (2 * low + core)]


def dw_product(here, attns, grads):
    cols = grads[0].shape[1]
    vmem = pl.BlockSpec(memory_space=pltpu.VMEM)
    return pl.pallas_call(
        dw_body,
        in_specs=[pl.BlockSpec(memory_space=pltpu.SMEM)] + [vmem] * 8,
        out_shape=[jax.ShapeDtypeStruct((4, 2, Z, BLK, BLK), BF16)] * 2,
        scratch_shapes=[
            pltpu.VMEM((Z * BLK, Y * BLK), BF16),
            pltpu.VMEM((Y * BLK, cols), BF16),
            pltpu.VMEM((4, 4, Z, BLK, BLK), BF16),
        ],
        compiler_params=params(),
        cost_estimate=cost(2 * 512 * 512 * cols, 2 * 512 * cols * 2),
        name="dw_product",
    )(here, *attns, *grads)


def mix_body(*refs):
    attn_refs, wide_ref, mix_refs, a_s = refs[:Z], refs[Z], refs[Z + 1 : Z + 1 + Y], refs[-1]
    for t in range(Z):
        for s in range(Y):
            a_s[s * BLK : (s + 1) * BLK, t * BLK : (t + 1) * BLK] = attn_refs[t][s]
    width = wide_ref.shape[1] // 4
    for j in range(4):
        cols = slice(j * width, (j + 1) * width)
        for s in range(Y):
            mix_refs[s][:, cols] = dot_nn(a_s[s * BLK : (s + 1) * BLK, :], wide_ref[:, cols]).astype(BF16)


def mix_product(attns, wide):
    cols = wide.shape[1]
    return pl.pallas_call(
        mix_body,
        out_shape=[jax.ShapeDtypeStruct((BLK, cols), BF16)] * Y,
        scratch_shapes=[pltpu.VMEM((Y * BLK, Z * BLK), BF16)],
        compiler_params=params(),
        cost_estimate=cost(2 * 512 * 512 * cols, 2 * 512 * cols * 2),
        name="mix_product",
    )(*attns, wide)


def fold_body(count, *refs):
    ins, outs = refs[:count], refs[count:]
    for i, out in enumerate(outs):
        total = ins[0][i].astype(F32)
        for part in ins[1:]:
            total = total + part[i].astype(F32)
        out[...] = total.astype(out.dtype)


def fold(parts, kind):
    shape = parts[0].shape
    return pl.pallas_call(
        functools.partial(fold_body, len(parts)),
        out_shape=[jax.ShapeDtypeStruct(shape[1:], kind)] * shape[0],
        compiler_params=params(),
        cost_estimate=cost(0, 5 * math.prod(shape) * 2),
        name="fold",
    )(*parts)


def place_mixed_body(here_ref, chosen_ref, p0, p1, p2, p3, out_ref):
    mine = pl.program_id(0) == half_of(here_ref, chosen_ref)

    @pl.when(mine)
    def _():
        total = p0[...].astype(F32) + p1[...].astype(F32) + p2[...].astype(F32) + p3[...].astype(F32)
        out_ref[0] = total.astype(BF16)

    @pl.when(jnp.logical_not(mine))
    def _():
        out_ref[...] = jnp.zeros(out_ref.shape, BF16)


def place_mixed(here, chosen, parts):
    cols = parts[0].shape[1]
    steps = 2
    width = cols // steps
    return pl.pallas_call(
        place_mixed_body,
        grid_spec=pltpu.PrefetchScalarGridSpec(
            num_scalar_prefetch=2,
            grid=(2, steps),
            in_specs=[pl.BlockSpec((BLK, width), lambda i, j, h, c: (0, j))] * Y,
            out_specs=pl.BlockSpec((1, BLK, width), lambda i, j, h, c: (0, i, j)),
        ),
        out_shape=jax.ShapeDtypeStruct((1, 2 * BLK, cols), BF16),
        compiler_params=params(),
        cost_estimate=cost(0, 6 * BLK * cols * 2),
        name="place_mixed",
    )(here, chosen, *parts)


def place_grads_body(here_ref, chosen_ref, back_ref, q_ref, k_ref, v_ref):
    mine = pl.program_id(0) == half_of(here_ref, chosen_ref)
    heads = back_ref.shape[0]

    @pl.when(mine)
    def _():
        for h in range(heads):
            cols = slice(h * BLK, (h + 1) * BLK)
            for part, out in enumerate((q_ref, k_ref, v_ref)):
                out[0, :, cols] = back_ref[h, part * BLK : (part + 1) * BLK, :]

    @pl.when(jnp.logical_not(mine))
    def _():
        for out in (q_ref, k_ref, v_ref):
            out[...] = jnp.zeros(out.shape, BF16)


def place_grads(here, chosen, back):
    feats = NC * BLK
    steps = 2
    width = feats // steps
    out = pl.BlockSpec((1, BLK, width), lambda i, j, h, c: (0, i, j))
    shape = jax.ShapeDtypeStruct((1, 2 * BLK, feats), BF16)
    return pl.pallas_call(
        place_grads_body,
        grid_spec=pltpu.PrefetchScalarGridSpec(
            num_scalar_prefetch=2,
            grid=(2, steps),
            in_specs=[pl.BlockSpec((NC // steps, 3 * BLK, BLK), lambda i, j, h, c: (j, 0, 0))],
            out_specs=[out] * 3,
        ),
        out_shape=[shape] * 3,
        compiler_params=params(),
        cost_estimate=cost(0, 9 * BLK * feats * 2),
        name="place_grads",
    )(here, chosen, back)


def along_y(x, s):
    return lax.ppermute(x, "ctx", [(c, c ^ (s * Z)) for c in range(NC)])


def along_z(x, t):
    return lax.ppermute(x, "ctx", [(c, c ^ t) for c in range(NC)])


def along_x(x, u):
    return lax.ppermute(x, "dp", [(d, d ^ (u * 4)) for d in range(16)])


def along_z_lo(x):
    return lax.ppermute(x, "dp", [(d, d ^ 2) for d in range(16)])


def along_core(x):
    return lax.ppermute(x, "dp", [(d, d ^ 1) for d in range(16)])


def spread(x, along):
    return [x] + [along(x, i) for i in (1, 2, 3)]


def swap(parts, along):
    return [parts[0]] + [along(parts[i], i) for i in (1, 2, 3)]


def shards(queries, keys, values, out_grad, chosen, proj):
    picked = chosen[0]
    ctx = lax.axis_index("ctx")
    dp = lax.axis_index("dp")
    here = jnp.stack([ctx, dp, ctx // Z, ctx % Z, dp // 4, dp % 4]).astype(jnp.int32)

    gs = take_grad(here, picked, out_grad)
    gs_y = spread(gs, along_y)
    qkv_own = take_heads(here, picked, queries, keys, values)

    rows_low = jnp.stack([proj, along_z_lo(proj)])
    rows_z, gs_y[1], gs_y[3], qkv_own = lax.optimization_barrier(
        (spread(rows_low, along_z), gs_y[1], gs_y[3], qkv_own)
    )
    rows_z = jnp.concatenate(rows_z, 0)
    rows_x = spread(rows_z, along_x)
    proj_rows = rows_x + [along_core(rows) for rows in rows_x]

    qkv = lax.all_to_all(qkv_own, "ctx", 0, 0, tiled=True)

    *grad_parts, wide = attn_grad_product(here, gs_y, proj_rows)
    grads = swap(grad_parts, along_z)
    qkv, grads[0] = lax.optimization_barrier((qkv, grads[0]))

    attn, *attn_parts, lse = attn_forward(here, picked, qkv)
    attns = swap(attn_parts, along_z)

    back = attn_backward(here, picked, qkv, grads, attn, lse)
    back, attns = lax.optimization_barrier((back, attns))
    back = lax.all_to_all(back, "ctx", 0, 0, tiled=True)

    dw_own, dw_other = dw_product(here, attns, gs_y)
    wide, dw_other = lax.optimization_barrier((wide, dw_other))
    mixed = swap(mix_product(attns, wide), along_y)
    dw = swap(fold([dw_own, along_core(dw_other)], BF16), along_x)
    dw_own, dw_other = fold(dw, BF16)
    dw = swap(fold([dw_own, along_z_lo(dw_other)], F32), along_z)

    attn_out = place_mixed(here, picked, mixed)
    placed = place_grads(here, picked, back)
    dw, (q_grad, k_grad, v_grad) = lax.optimization_barrier((dw, placed))
    proj_grad = dw[0] + dw[1] + dw[2] + dw[3]
    return attn_out, q_grad, k_grad, v_grad, proj_grad


def solution(mesh):
    rows = P("dp", "ctx", None)
    return jax.shard_map(
        shards,
        mesh=mesh,
        in_specs=(rows, rows, rows, rows, P("dp", None), P("ctx", "dp")),
        out_specs=(rows, rows, rows, rows, P("ctx", "dp")),
        check_vma=False,
    )
```
